256 devices in a mesh: phase: 8 (over z), ctx: 16 (over x, y), tp: 2 (over core).
Axes of the slice: x: 4, y: 4, z: 8, core: 2. Of those that a mesh axis runs over, the one named last changes fastest.
Arguments:
- hidden_in: bfloat16 [1, 2048, 3072], P(None, 'ctx', 'tp'), may hold values from -48 to 48
- qkv_weight: bfloat16 [8, 32, 96, 288], P('phase', 'tp'), may hold values from -0.625 to 0.625
- log_decay: float32 [8, 1, 2048, 32], P('phase', None, 'ctx', 'tp'), may hold values from -0.6 to 0
- lengths: int32 [1, 4], replicated, may hold values from 1 to 1536, 2048 in all within a row
- out_mantissa: bfloat16 [8, 3072, 3072], P('phase', 'ctx', 'tp'), may hold values from -0.109375 to 0.109375
- out_exponent: int32 [8, 32, 32], P('phase', None, 'tp'), may hold values from -3 to 1
Outputs:
- outputs: bfloat16 [8, 1, 2048, 3072], P('phase', None, 'ctx', 'tp')
The draws below stay inside these ranges and needn't reach their ends.
Inputs may be any that keep to these rules, and one draw needn't show every extreme that they name: lengths[m] lists the 4 prompt lengths packed in micro-batch m in order; they sum to 2048 and the largest is exactly 1536.
All inputs are finite; a program needn't handle non-finite values.
Results may differ from the reference program's by a relative error of at most 0.034.
Values may be sent and summed in bfloat16 or wider, within the bound.
A program may use at most 128 MiB of HBM per device.

```python
import math
import jax
import jax.numpy as jnp
import numpy as np
from jax import lax

HEADS = 32
HEAD = 96
D = 3072
SPAN = 128
MICRO_BATCHES = 1
PROMPTS = 4
LAYER_COUNT = 8
SEQUENCE_LENGTH = 2048
MOST = 1536


def draw_hidden_in(key, part):
    key = jax.random.fold_in(key, 11)
    key_matrix = jax.random.split(key, 3)
    shape = (MICRO_BATCHES, SEQUENCE_LENGTH, D)
    columns = jnp.arange(D, dtype=jnp.float32) / D
    col_scale = jnp.exp(columns * math.log(3.0) + jax.random.uniform(key_matrix[1], (D,), jnp.float32, math.log(0.5), math.log(2.0)))
    row_scale = jnp.exp(jax.random.uniform(key_matrix[2], (MICRO_BATCHES, SEQUENCE_LENGTH, 1), jnp.float32, math.log(0.5), math.log(2.0)))
    base = jax.random.truncated_normal(key_matrix[0], -4.0, 4.0, shape, jnp.float32)
    return (base * row_scale * col_scale).astype(jnp.bfloat16)


def draw_log_decay(key, part):
    key = jax.random.fold_in(key, 17)
    key_matrix = jax.random.split(key, 6)
    share = 0.5
    head_shape = (LAYER_COUNT, 1, 1, HEADS)
    full_shape = (LAYER_COUNT, MICRO_BATCHES, SEQUENCE_LENGTH, HEADS)
    slow = jax.random.uniform(key_matrix[0], head_shape, jnp.float32) < share
    slow_rate = jnp.exp(jax.random.uniform(key_matrix[1], head_shape, jnp.float32, math.log(0.05 / SEQUENCE_LENGTH), math.log(0.3 / SEQUENCE_LENGTH)))
    fast_rate = jnp.exp(jax.random.uniform(key_matrix[2], head_shape, jnp.float32, math.log(1.0 / 50.0), math.log(1.0 / 25.0)))
    decay_speed = jnp.where(slow, slow_rate, fast_rate)
    multiplier = jnp.exp(jax.random.uniform(key_matrix[3], full_shape, jnp.float32, math.log(0.5), math.log(2.0)))
    spike_position = jax.random.randint(key_matrix[4], (LAYER_COUNT, MICRO_BATCHES, SEQUENCE_LENGTH, 1), 0, SEQUENCE_LENGTH) < 3
    training_loss = jax.random.uniform(key_matrix[5], full_shape, jnp.float32, 0.2, 0.4)
    spike_events = jnp.where(spike_position, jnp.log(1.0 - training_loss), jnp.zeros_like(training_loss))
    return (-decay_speed * multiplier + spike_events).astype(jnp.float32)


def place_ends(entries, own_key, least, largest):
    longest = entries.shape.index(max(entries.shape))
    spots = []
    for shift in (0, 1):
        where = [jax.random.randint(jax.random.fold_in(own_key, axis), (), 0, length) for axis, length in enumerate(entries.shape)]
        where[longest] = (where[longest] + shift) % entries.shape[longest]
        spots.append(tuple(where))
    return entries.at[spots[0]].set(least).at[spots[1]].set(largest)


def level_of(rng, dims, shards, least, largest):
    def one(axis_at, blocks):
        heights = jax.random.uniform(jax.random.fold_in(jax.random.fold_in(rng, 6), axis_at), (blocks,), jnp.float32, least / len(shards), largest / len(shards))
        return jnp.repeat(jnp.exp(heights), dims[axis_at] // blocks).reshape((-1,) + (1,) * (len(dims) - axis_at - 1))

    loudness = one(*shards[0])
    for cut in shards[1:]:
        loudness = loudness * one(*cut)
    return loudness


def profile(count, total, bound, slope):
    weights = [(1 << 20) // math.isqrt(rank ** slope) + 1 for rank in range(2, count + 1)]
    spare, given = total - bound - (count - 1), [1] * (count - 1)
    while spare > 0:
        candidates = [i for i in range(count - 1) if given[i] < bound]
        mass, budget = sum([weights[i] for i in candidates]), spare
        for i in candidates:
            extra = min(bound - given[i], max(1, budget * weights[i] // mass), spare)
            given[i] = given[i] + extra
            spare = spare - extra
    return np.array([bound] + given)


def ragged_sizes(key, amount, total, bound, slope):
    if amount == 2:
        one = jax.random.randint(key, (), max(1, total - bound), min(bound, total - 1) + 1)
        return jnp.stack([one, total - one])
    sizes = jnp.asarray(profile(amount, total, bound, slope), jnp.int32)
    pairs = (amount - 1) // 2
    donor, sink = sizes[1:1 + 2 * pairs:2], sizes[2:2 + 2 * pairs:2]
    margin = jnp.minimum(donor - 1, bound - sink)
    shifted = jax.random.randint(jax.random.fold_in(key, 1), (pairs,), 0, 1 << 20) % (margin + 1)
    sizes = sizes.at[1:1 + 2 * pairs:2].set(donor - shifted).at[2:2 + 2 * pairs:2].set(sink + shifted)
    return sizes[jax.random.permutation(jax.random.fold_in(key, 2), amount)]


def centred(own_key, shape, scale, reach, cuts=(), held_as=jnp.bfloat16):
    values = scale * jax.random.normal(own_key, shape, jnp.float32)
    if cuts:
        values = values * level_of(own_key, shape, cuts, -0.22, 0.18)
    return jnp.clip(values, -reach, reach).astype(held_as)


def setup_inputs(seed: int = 0) -> dict:
    key_of = jax.random.split(jax.random.key(seed), 7)
    return {
        "hidden_in": draw_hidden_in(jax.random.fold_in(key_of[6], 71), 0),
        "qkv_weight": centred(key_of[1], (LAYER_COUNT, HEADS, HEAD, 3 * HEAD), HEAD ** -0.5, 0.625, ((0, 8), (1, 2))),
        "log_decay": draw_log_decay(jax.random.fold_in(key_of[6], 71), 0),
        "lengths": jax.vmap(lambda own: ragged_sizes(own, PROMPTS, SEQUENCE_LENGTH, MOST, 2))(jax.random.split(key_of[3], MICRO_BATCHES)).reshape((MICRO_BATCHES, PROMPTS)).astype(jnp.int32),
        "out_mantissa": centred(key_of[4], (LAYER_COUNT, D, D), D ** -0.5, 0.109375, ((0, 8), (1, 16), (2, 2))),
        "out_exponent": place_ends(jax.random.randint(key_of[5], (LAYER_COUNT, HEADS, HEADS), -3, 2), jax.random.fold_in(key_of[5], 1), -3, 1).astype(jnp.int32),
    }


epsilon = 1e-05

def dequantize(mantissa, exponent, head_size):
    scale = jnp.exp2(exponent.astype(jnp.float32))
    blocks = mantissa.astype(jnp.float32).reshape(exponent.shape[0], head_size, exponent.shape[1], head_size)
    return (blocks * scale[:, None, :, None]).reshape(mantissa.shape).astype(jnp.bfloat16)

def segment_ids(lengths_row, positions):
    ends = jnp.cumsum(lengths_row)[:-1].astype(jnp.int32)
    return lax.optimization_barrier(jnp.sum((positions[:, None] >= ends[None, :]).astype(jnp.int32), axis=1)).astype(jnp.int32)

def block_terms(query_rows, key_rows, value_rows, decayed, segment, before):
    count = segment.shape[0]
    places = jnp.arange(count)
    allowed = (places[None, :] <= places[:, None]) & (segment[None, :] == segment[:, None])
    spread = decayed[:, :, None] - decayed[:, None, :]
    multiplier = jnp.exp(jnp.where(allowed[None], spread, -1e+30))
    scores = jnp.einsum('hid,hjd->hij', query_rows.astype(jnp.float32), key_rows.astype(jnp.float32))
    weights = lax.optimization_barrier((scores * multiplier).astype(jnp.bfloat16))
    inner = jnp.einsum('hij,hjd->hid', weights.astype(jnp.float32), value_rows.astype(jnp.float32))
    final = decayed[:, -1]
    in_last = (segment == segment[-1]).astype(jnp.float32)
    key_scale = jnp.exp(final[:, None] - decayed) * in_last[None, :]
    keyed = lax.optimization_barrier((key_rows.astype(jnp.float32) * key_scale[:, :, None]).astype(jnp.bfloat16))
    own = jnp.einsum('hjd,hje->hde', keyed.astype(jnp.float32), value_rows.astype(jnp.float32))
    carry_on = jnp.where(segment[-1] == before, jnp.exp(final), jnp.zeros_like(final))
    continues = (segment == before).astype(jnp.float32)
    query_scale = jnp.exp(decayed) * continues[None, :]
    queried = lax.optimization_barrier((query_rows.astype(jnp.float32) * query_scale[:, :, None]).astype(jnp.bfloat16))
    return (inner, own, carry_on, queried)

def finish(inner, queried, state):
    state_b = lax.optimization_barrier(state.astype(jnp.bfloat16))
    attended = inner + jnp.einsum('hid,hde->hie', queried.astype(jnp.float32), state_b.astype(jnp.float32))
    scale = lax.rsqrt(lax.optimization_barrier(jnp.mean(attended * attended, axis=2, keepdims=True)) + epsilon)
    normed = (attended * scale).astype(jnp.bfloat16)
    return normed.transpose(1, 0, 2).reshape(normed.shape[1], -1)

def layer(hidden, qkv_layer, decay_layer, segment, out_weight):
    seq_len, width = hidden.shape
    current = hidden.astype(jnp.float32)
    inverse = lax.rsqrt(lax.optimization_barrier(jnp.mean(current * current, axis=1)) + epsilon)
    normed = lax.optimization_barrier((current * inverse[:, None]).astype(jnp.bfloat16))
    head_rows = normed.astype(jnp.float32).reshape(seq_len, HEADS, HEAD)
    project = jnp.einsum('rhd,hde->hre', head_rows, qkv_layer.astype(jnp.float32))
    query_rows = lax.optimization_barrier(jax.nn.silu(project[:, :, :HEAD]).astype(jnp.bfloat16))
    key_rows = lax.optimization_barrier(jax.nn.silu(project[:, :, HEAD:2 * HEAD]).astype(jnp.bfloat16))
    value_rows = lax.optimization_barrier(project[:, :, 2 * HEAD:].astype(jnp.bfloat16))
    count = seq_len // SPAN

    def split(array):
        return array.reshape(HEADS, count, SPAN, HEAD).transpose(1, 0, 2, 3)
    decay_blocks = decay_layer.T.reshape(HEADS, count, SPAN).transpose(1, 0, 2)
    decayed = jnp.cumsum(decay_blocks, axis=2)
    seg_blocks = segment.reshape(count, SPAN)
    before = jnp.concatenate([jnp.full((1,), -1, jnp.int32), seg_blocks[:-1, -1].astype(jnp.int32)]).astype(jnp.int32)

    def advance(state, parts):
        query_b, key_b, value_b, decay_b, seg_b, before_b = parts
        inner, own, carry_on, queried = block_terms(query_b, key_b, value_b, decay_b, seg_b, before_b)
        rows_out = finish(inner, queried, state)
        return (carry_on[:, None, None] * state + own, rows_out)
    start = jnp.zeros((HEADS, HEAD, HEAD), jnp.float32)
    _, rows_all = lax.scan(advance, start, (split(query_rows), split(key_rows), split(value_rows), decayed, seg_blocks, before))
    attended = rows_all.reshape(seq_len, width)
    mixed = jnp.dot(attended, out_weight, preferred_element_type=jnp.float32)
    return (current + mixed).astype(jnp.bfloat16)

def reference(hidden_in, qkv_weight, log_decay, lengths, out_mantissa, out_exponent):
    positions = jnp.arange(SEQUENCE_LENGTH, dtype=jnp.int32)
    weights_eff = [dequantize(out_mantissa[index], out_exponent[index], HEAD) for index in range(LAYER_COUNT)]
    collected = [[None] * MICRO_BATCHES for index in range(LAYER_COUNT)]
    for micro_index in range(MICRO_BATCHES):
        segment = segment_ids(lengths[micro_index], positions)
        hidden = hidden_in[micro_index]
        for layer_index in range(LAYER_COUNT):
            hidden = layer(hidden, qkv_weight[layer_index], log_decay[layer_index, micro_index], segment, weights_eff[layer_index])
            collected[layer_index][micro_index] = hidden
    return jnp.stack([jnp.stack(group) for group in collected])
```

```python
import jax
import jax.numpy as jnp
from jax import lax
from jax.experimental import pallas as pl
from jax.experimental.pallas import tpu as pltpu
from jax.sharding import PartitionSpec as P

EPSILON = 1e-05
MESH = pl.DeviceIdType.MESH
LAYERS = 8
BLOCKS = 16
ROWS = 128
HEAD = 96
OWN = 4
WIDE = OWN * HEAD
MODEL = 3072
F32 = jnp.float32
BF16 = jnp.bfloat16


def contract(a, b, da, db):
    return lax.dot_general(a, b, (((da,), (db,)), ((), ())), preferred_element_type=F32)


def kernel(
    hid, wd, qk, ld, lens, out,
    xbuf, sbuf, nbuf, tbuf, wbuf, qbuf, graw, gbuf, cbuf, mbuf, wst, qst, wsrc, qsrc,
    bits, ldsend, hsem, sibsend, sibsem, gsem, csend, csem,
    ssend, ssem, tsend, tsem, nsend, nsem, osend, osem,
    zsend, zsem, rsend, wsem, qsem,
):
    z, c, t = lax.axis_index("phase"), lax.axis_index("ctx"), lax.axis_index("tp")
    y = lax.rem(c, 4)
    zq, zr = z // 4, lax.rem(z, 4)

    def push(src, dst, s, r, dev):
        return pltpu.make_async_remote_copy(
            src_ref=src, dst_ref=dst, send_sem=s, recv_sem=r, device_id=dev, device_id_type=MESH
        )

    def arrived(dst, r):
        push(dst, dst, r, r, (z, c, 1 - t)).wait_recv()

    def sent(src, s):
        push(src, src, s, s, (z, c, 1 - t)).wait_send()

    def cols(ref, k):
        return ref.at[:, pl.ds(pl.multiple_of(WIDE * k, 128), WIDE)]

    barrier = pltpu.get_barrier_semaphore()

    def greet(dev):
        pl.semaphore_signal(barrier, inc=1, device_id=dev, device_id_type=MESH)

    greet((z, c, 1 - t))
    for d in range(1, LAYERS):
        for core in range(2):
            greet((lax.rem(z + d, LAYERS), c, core))

    def greet_plane(d, carry):
        there = lax.rem(c + d, BLOCKS)
        greet((z, there, 1))

        @pl.when(t == 1)
        def _():
            greet((z, there, 0))

        return carry

    lax.fori_loop(1, BLOCKS, greet_plane, 0)

    @pl.when(t == 1)
    def _():
        pl.semaphore_wait(barrier, 45)

    @pl.when(t == 0)
    def _():
        pl.semaphore_wait(barrier, 30)

    hid_local = pltpu.make_async_copy(cols(hid, zr), xbuf, hsem)
    hid_remote = push(cols(hid, zr), xbuf, sibsend.at[6], hsem, (z, c, 1))

    @pl.when((t == 1) & (zq == 1))
    def _():
        hid_local.start()

    @pl.when((t == 0) & (zq == 0))
    def _():
        hid_remote.start()

    for k in range(4):
        mine = (t == 1) & (zq == 1) & (zr == k)

        @pl.when(mine)
        def _():
            pltpu.make_async_copy(ld.at[k], graw.at[z], gsem.at[z]).start()

        @pl.when(jnp.logical_not(mine))
        def _():
            push(ld.at[k], graw.at[z], ldsend.at[k], gsem.at[z], (4 * t + k, c, 1)).start()

    @pl.when(t == 0)
    def _():
        distribute(z, c, y, zq, zr, push, arrived, sent, cols, wd, qk, wst, qst, wsrc, qsrc, wbuf, qbuf,
                   sibsem, zsend, zsem, rsend, wsem, qsem)

    @pl.when(t == 1)
    def _():
        for k in range(4):
            push(qk.at[4 * k + y], qsrc.at[k], sibsend.at[k], sibsem.at[k], (z, c, 0)).start()
        push(wd, wsrc, sibsend.at[4], sibsem.at[4], (z, c, 0)).start()
        layers(z, c, zq, zr, push, arrived, sent, cols, hid_local, hid_remote, lens, out,
               xbuf, sbuf, nbuf, tbuf, wbuf, qbuf, graw, gbuf, cbuf, mbuf, bits,
               gsem, csend, csem, ssend, ssem, tsend, tsem, nsend, nsem, osend, osem, wsem, qsem)
        for k in range(4):
            sent(qsrc.at[k], sibsend.at[k])
        sent(wsrc, sibsend.at[4])

    @pl.when((t == 0) & (zq == 0))
    def _():
        hid_remote.wait_send()

    for k in range(4):
        mine = (t == 1) & (zq == 1) & (zr == k)

        @pl.when(jnp.logical_not(mine))
        def _():
            sent(ld.at[k], ldsend.at[k])
            arrived(cols(out, k), osem.at[k])


def distribute(z, c, y, zq, zr, push, arrived, sent, cols, wd, qk, wst, qst, wsrc, qsrc, wbuf, qbuf,
               sibsem, zsend, zsem, rsend, wsem, qsem):
    base = c - y
    for k in range(4):
        arrived(qsrc.at[k], sibsem.at[k])
    arrived(wsrc, sibsem.at[4])

    def step(l, carry):
        @pl.when(z == l)
        def _():
            for kind in range(2):
                for d in (4, 3, 5, 2, 6, 1, 7, 0):
                    there = lax.rem(z + d, LAYERS)
                    k = lax.rem(there, 4)
                    for half in range(2):

                        @pl.when(there // 4 == half)
                        def _():
                            if kind == 0:
                                src = qsrc.at[k] if half else qk.at[4 * k + y]
                                dst = qst.at[l]
                            else:
                                src = cols(wsrc if half else wd, k)
                                dst = wst.at[l]
                            if d:
                                push(src, dst, zsend.at[kind, d], zsem.at[kind, l], (there, c, 0)).start()
                            else:
                                pltpu.make_async_copy(src, dst, zsem.at[kind, l]).start()

        @pl.when(z == l)
        def _():
            pltpu.make_async_copy(qst.at[l], qst.at[l], zsem.at[0, l]).wait()

        @pl.when(z != l)
        def _():
            arrived(qst.at[l], zsem.at[0, l])

        for yy in range(4):
            push(qst.at[l], qbuf.at[l, y], rsend.at[16 + yy], qsem.at[l, y], (z, base + yy, 1)).start()

        @pl.when(z == l)
        def _():
            pltpu.make_async_copy(wst.at[l], wst.at[l], zsem.at[1, l]).wait()

        @pl.when(z != l)
        def _():
            arrived(wst.at[l], zsem.at[1, l])

        def relay(d, carry):
            there = lax.rem(c + d, BLOCKS)
            push(wst.at[l], wbuf.at[l, c], rsend.at[d], wsem.at[l, c], (z, there, 1)).start()
            return carry

        lax.fori_loop(0, BLOCKS, relay, 0)
        for yy in range(4):
            sent(qst.at[l], rsend.at[16 + yy])

        def relayed(d, carry):
            sent(wst.at[l], rsend.at[d])
            return carry

        lax.fori_loop(0, BLOCKS, relayed, 0)

        @pl.when(z == l)
        def _():
            for d in range(1, LAYERS):
                sent(qst.at[l], zsend.at[0, d])
                sent(wst.at[l], zsend.at[1, d])

        return carry

    lax.fori_loop(0, LAYERS, step, 0)


def layers(z, c, zq, zr, push, arrived, sent, cols, hid_local, hid_remote, lens, out,
           xbuf, sbuf, nbuf, tbuf, wbuf, qbuf, graw, gbuf, cbuf, mbuf, bits,
           gsem, csend, csem, ssend, ssem, tsend, tsem, nsend, nsem, osend, osem, wsem, qsem):
    e1 = lens[0, 0]
    e2 = e1 + lens[0, 1]
    e3 = e2 + lens[0, 2]

    def segment(p):
        return (p >= e1).astype(jnp.int32) + (p >= e2).astype(jnp.int32) + (p >= e3).astype(jnp.int32)

    first = c * ROWS
    seg_row = segment(first + lax.broadcasted_iota(jnp.int32, (ROWS, ROWS), 1))
    seg_col = segment(first + lax.broadcasted_iota(jnp.int32, (ROWS, ROWS), 0))
    later = lax.broadcasted_iota(jnp.int32, (ROWS, ROWS), 0) <= lax.broadcasted_iota(jnp.int32, (ROWS, ROWS), 1)
    small = first + lax.broadcasted_iota(jnp.int32, (8, ROWS), 1)
    seg_small = segment(small)
    seg_last = segment(jnp.full((8, ROWS), first + ROWS - 1, jnp.int32))
    before = jnp.where(c == 0, jnp.full((8, ROWS), -1, jnp.int32), segment(jnp.full((8, ROWS), first - 1, jnp.int32)))
    bits[0] = (seg_small == seg_last).astype(F32)
    bits[1] = (seg_small == before).astype(F32)
    bits[2] = (seg_last == before).astype(F32)
    lane8 = lax.broadcasted_iota(jnp.int32, (8, ROWS), 1)

    for l in range(LAYERS):
        mine = (zq == 1) & (z == l)

        @pl.when(mine)
        def _():
            pltpu.make_async_copy(graw.at[l], graw.at[l], gsem.at[l]).wait()

        @pl.when(jnp.logical_not(mine))
        def _():
            arrived(graw.at[l], gsem.at[l])

    def decays(l, carry):
        g = graw[l]
        for s in (1, 2, 4, 8, 16, 32, 64):
            g = g + jnp.where(lane8 >= s, pltpu.roll(g, s, 1), 0.0)
        gbuf[l] = g
        kept = jnp.exp(jnp.broadcast_to(g[:, ROWS - 1 :], (8, ROWS))) * bits[2]
        cbuf[c, l] = jnp.where(lane8 < HEAD, kept, jnp.broadcast_to(kept[3:4], (8, ROWS)))
        return carry

    lax.fori_loop(0, LAYERS, decays, 0)

    def tell(there, carry):
        push(cbuf.at[c], cbuf.at[c], csend.at[there], csem.at[c], (z, there, 1)).start()
        return carry

    lax.fori_loop(c + 1, BLOCKS, tell, 0)
    allowed = later & (seg_row == seg_col)

    def masks(l, carry):
        for h in range(OWN):
            row = jnp.broadcast_to(gbuf[l, h : h + 1], (ROWS, ROWS))
            mbuf[l, h] = jnp.exp(jnp.where(allowed, row - row.T, -1e30))
        return carry

    lax.fori_loop(0, LAYERS, masks, 0)

    @pl.when(zq == 1)
    def _():
        hid_local.wait()

    @pl.when(zq == 0)
    def _():
        hid_remote.wait_recv()

    def heard(there, carry):
        arrived(cbuf.at[there], csem.at[there])
        return carry

    lax.fori_loop(0, c, heard, 0)
    lane96 = lax.broadcasted_iota(jnp.int32, (HEAD, ROWS), 1)

    def emit(l):
        self_kept = (zq == 1) & (z == l)

        @pl.when(self_kept)
        def _():
            pltpu.make_async_copy(xbuf, cols(out, zr), osem.at[zr]).start()

        @pl.when(jnp.logical_not(self_kept))
        def _():
            push(xbuf, cols(out, zr), osend, osem.at[zr], (l, c, zq)).start()

    def emitted(l):
        self_kept = (zq == 1) & (z == l)

        @pl.when(self_kept)
        def _():
            pltpu.make_async_copy(xbuf, cols(out, zr), osem.at[zr]).wait()

        @pl.when(jnp.logical_not(self_kept))
        def _():
            sent(xbuf, osend)

    def layer(l, carry):
        x = xbuf[...]
        xt = x.astype(F32).T
        own_squares = jnp.sum(xt * xt, axis=0, keepdims=True)
        sbuf[l, z] = own_squares
        for d in (4, 3, 5, 2, 6, 1, 7):
            push(sbuf.at[l, z], sbuf.at[l, z], ssend.at[d], ssem.at[l, z], (lax.rem(z + d, LAYERS), c, 1)).start()
        for h in range(OWN):
            arrived(qbuf.at[l, h], qsem.at[l, h])
        squares = own_squares
        for d in (1, 7, 2, 6, 3, 5, 4):
            there = lax.rem(z + d, LAYERS)
            arrived(sbuf.at[l, there], ssem.at[l, there])
            squares = squares + sbuf[l, there]
        xtb = (xt * lax.rsqrt(squares / MODEL + EPSILON)).astype(BF16)
        raw = [contract(qbuf[l, h], xtb[HEAD * h : HEAD * h + HEAD], 1, 0) for h in range(OWN)]

        @pl.when(l > 0)
        def _():
            emit(l - 1)

        g = gbuf[l]
        key_scale = jnp.exp(jnp.broadcast_to(g[:, ROWS - 1 :], (8, ROWS)) - g) * bits[0]
        query_scale = jnp.exp(g) * bits[1]
        keys, values, keyed = [], [], []
        for h in range(OWN):
            k = jax.nn.silu(raw[h][HEAD : 2 * HEAD]).astype(BF16)
            keys.append(k)
            values.append(raw[h][2 * HEAD :].astype(BF16))
            keyed.append((k.astype(F32) * key_scale[h : h + 1]).astype(BF16))
        for p in range(3):
            right = jnp.concatenate([keyed[p], keyed[3][32 * p : 32 * p + 32]], axis=0)
            both = contract(jnp.concatenate([values[p], values[3]], axis=0), right, 1, 1)
            tbuf[l, c, HEAD * p : HEAD * p + HEAD] = jnp.where(lane96 < HEAD, both[:HEAD], both[HEAD:]).astype(BF16)

        def states_out(there, carry):
            push(tbuf.at[l, c], tbuf.at[l, c], tsend.at[there], tsem.at[l, c], (z, there, 1)).start()
            return carry

        lax.fori_loop(c + 1, BLOCKS, states_out, 0)

        inner, queried = [], []
        for h in range(OWN):
            q = jax.nn.silu(raw[h][:HEAD]).astype(BF16)
            scores = contract(keys[h], q, 0, 0)
            weights = (scores * mbuf[l, h]).astype(BF16)
            inner.append(contract(values[h], weights, 1, 0))
            queried.append((q.astype(F32) * query_scale[h : h + 1]).astype(BF16))

        def fold(there, state):
            arrived(tbuf.at[l, there], tsem.at[l, there])
            return tuple(
                s * cbuf[there, l, p : p + 1] + tbuf[l, there, HEAD * p : HEAD * p + HEAD].astype(F32)
                for p, s in enumerate(state)
            )

        state = lax.fori_loop(0, c, fold, tuple(jnp.zeros((HEAD, ROWS), F32) for _ in range(3)))
        attended = list(inner)
        for p in range(3):
            left = jnp.concatenate([queried[p], jnp.zeros((32, ROWS), BF16)], axis=0)
            right = jnp.concatenate([jnp.zeros((HEAD, ROWS), BF16), queried[3][32 * p : 32 * p + 32]], axis=0)
            both = contract(state[p].astype(BF16), jnp.concatenate([left, right], axis=1), 1, 0)
            attended[p] = attended[p] + both[:, :ROWS]
            attended[3] = attended[3] + both[:, ROWS:]
        normed = [a * lax.rsqrt(jnp.mean(a * a, axis=0, keepdims=True) + EPSILON) for a in attended]
        nbuf[l, z] = jnp.concatenate(normed, axis=0).T.astype(BF16)
        for d in (4, 3, 5, 2, 6, 1, 7):
            push(nbuf.at[l, z], nbuf.at[l, z], nsend.at[d], nsem.at[l, z], (lax.rem(z + d, LAYERS), c, 1)).start()

        total = x.astype(F32)
        for d in (0, 1, 7, 2, 6, 3, 5, 4):
            there = lax.rem(z + d, LAYERS)
            for half in range(2):
                arrived(wbuf.at[l, 2 * there + half], wsem.at[l, 2 * there + half])
            if d:
                arrived(nbuf.at[l, there], nsem.at[l, there])
            weight = wbuf[l, pl.ds(2 * there, 2)].reshape(WIDE, WIDE)
            total = total + contract(nbuf[l, there], weight, 1, 0)

        @pl.when(l > 0)
        def _():
            emitted(l - 1)

        xbuf[...] = total.astype(BF16)
        for d in range(1, LAYERS):
            sent(sbuf.at[l, z], ssend.at[d])
            sent(nbuf.at[l, z], nsend.at[d])

        def states_sent(there, carry):
            sent(tbuf.at[l, c], tsend.at[there])
            return carry

        lax.fori_loop(c + 1, BLOCKS, states_sent, 0)
        return carry

    lax.fori_loop(0, LAYERS, layer, 0)
    emit(LAYERS - 1)
    emitted(LAYERS - 1)

    def told(there, carry):
        sent(cbuf.at[c], csend.at[there])
        return carry

    lax.fori_loop(c + 1, BLOCKS, told, 0)


def shards(hidden_in, qkv_weight, log_decay, lengths, out_mantissa, out_exponent):
    ctx = lax.axis_index("ctx")
    exponent = lax.dynamic_slice_in_dim(out_exponent[0], 2 * ctx, 2, 0)
    scale = jnp.exp2(exponent.astype(F32))
    scale = jnp.repeat(scale, HEAD, axis=1)[:, None, :]
    weight = (out_mantissa[0].astype(F32).reshape(2, HEAD, -1) * scale).reshape(2 * HEAD, -1).astype(BF16)
    qkv = qkv_weight[0].swapaxes(1, 2)
    decay = jnp.pad(log_decay[0, 0].T.reshape(4, OWN, ROWS), ((0, 0), (0, 8 - OWN), (0, 0)))
    half = hidden_in.shape[2]
    dma = pltpu.SemaphoreType.DMA
    anywhere = pl.BlockSpec(memory_space=pl.ANY)
    outputs = pl.pallas_call(
        kernel,
        out_shape=jax.ShapeDtypeStruct((ROWS, half), BF16),
        in_specs=[anywhere] * 4 + [pl.BlockSpec(memory_space=pltpu.SMEM)],
        out_specs=anywhere,
        scratch_shapes=[
            pltpu.VMEM((ROWS, WIDE), BF16),
            pltpu.VMEM((LAYERS, LAYERS, 1, ROWS), F32),
            pltpu.VMEM((LAYERS, LAYERS, ROWS, WIDE), BF16),
            pltpu.VMEM((LAYERS, BLOCKS, 3 * HEAD, ROWS), BF16),
            pltpu.VMEM((LAYERS, BLOCKS, 2 * HEAD, WIDE), BF16),
            pltpu.VMEM((LAYERS, OWN, 3 * HEAD, HEAD), BF16),
            pltpu.VMEM((LAYERS, 8, ROWS), F32),
            pltpu.VMEM((LAYERS, 8, ROWS), F32),
            pltpu.VMEM((BLOCKS, LAYERS, 8, ROWS), F32),
            pltpu.VMEM((LAYERS, OWN, ROWS, ROWS), F32),
            pltpu.VMEM((LAYERS, 2 * HEAD, WIDE), BF16),
            pltpu.VMEM((LAYERS, 3 * HEAD, HEAD), BF16),
            pltpu.VMEM((2 * HEAD, half), BF16),
            pltpu.VMEM((4, 3 * HEAD, HEAD), BF16),
            pltpu.VMEM((3, 8, ROWS), F32),
            dma((4,)),
            dma,
            dma((7,)),
            dma((5,)),
            dma((LAYERS,)),
            dma((BLOCKS,)),
            dma((BLOCKS,)),
            dma((LAYERS,)),
            dma((LAYERS, LAYERS)),
            dma((BLOCKS,)),
            dma((LAYERS, BLOCKS)),
            dma((LAYERS,)),
            dma((LAYERS, LAYERS)),
            dma,
            dma((4,)),
            dma((2, LAYERS)),
            dma((2, LAYERS)),
            dma((20,)),
            dma((LAYERS, BLOCKS)),
            dma((LAYERS, OWN)),
        ],
        compiler_params=pltpu.CompilerParams(collective_id=0, has_side_effects=True, vmem_limit_bytes=58 << 20),
    )(hidden_in[0], weight, qkv, decay, lengths)
    return outputs[None, None]


def solution(mesh):
    in_specs = (
        P(None, "ctx", "tp"),
        P("phase", "tp", None, None),
        P("phase", None, "ctx", "tp"),
        P(),
        P("phase", "ctx", "tp"),
        P("phase", None, "tp"),
    )
    out_specs = P("phase", None, "ctx", "tp")
    return jax.shard_map(shards, mesh=mesh, in_specs=in_specs, out_specs=out_specs, check_vma=False)
```

```python
import jax
import jax.numpy as jnp
from jax import lax
from jax.experimental import pallas as pl
from jax.experimental.pallas import tpu as pltpu
from jax.sharding import PartitionSpec as P

EPSILON = 1e-05
MESH = pl.DeviceIdType.MESH
LAYERS = 8
BLOCKS = 16
ROWS = 128
HEAD = 96
OWN = 4
WIDE = OWN * HEAD
MODEL = 3072
F32 = jnp.float32
BF16 = jnp.bfloat16


def contract(a, b, da, db):
    return lax.dot_general(a, b, (((da,), (db,)), ((), ())), preferred_element_type=F32)


def kernel(
    hid, wd, qk, ld, lens, out,
    xbuf, sbuf, nbuf, tbuf, wbuf, qbuf, graw, gbuf, cbuf, mbuf, wst, qst, wsrc, qsrc,
    bits, ldsend, hsem, sibsend, sibsem, gsem, csend, csem,
    ssend, ssem, tsend, tsem, nsend, nsem, osend, osem,
    zsend, zsem, psend, psem, rsend, wsem, qsem,
):
    z, c, t = lax.axis_index("phase"), lax.axis_index("ctx"), lax.axis_index("tp")
    y = lax.rem(c, 4)
    zq, zr = z // 4, lax.rem(z, 4)

    def push(src, dst, s, r, dev):
        return pltpu.make_async_remote_copy(
            src_ref=src, dst_ref=dst, send_sem=s, recv_sem=r, device_id=dev, device_id_type=MESH
        )

    def arrived(dst, r):
        push(dst, dst, r, r, (z, c, 1 - t)).wait_recv()

    def sent(src, s):
        push(src, src, s, s, (z, c, 1 - t)).wait_send()

    def cols(ref, k):
        return ref.at[:, pl.ds(pl.multiple_of(WIDE * k, 128), WIDE)]

    barrier = pltpu.get_barrier_semaphore()

    def greet(dev):
        pl.semaphore_signal(barrier, inc=1, device_id=dev, device_id_type=MESH)

    greet((z, c, 1 - t))
    for d in range(1, LAYERS):
        for core in range(2):
            greet((lax.rem(z + d, LAYERS), c, core))

    def greet_plane(d, carry):
        for core in range(2):
            greet((z, lax.rem(c + d, BLOCKS), core))
        return carry

    lax.fori_loop(1, BLOCKS, greet_plane, 0)
    pl.semaphore_wait(barrier, 2 * (LAYERS + BLOCKS) - 3)

    hid_local = pltpu.make_async_copy(cols(hid, zr), xbuf, hsem)
    hid_remote = push(cols(hid, zr), xbuf, sibsend.at[6], hsem, (z, c, 1))

    @pl.when((t == 1) & (zq == 1))
    def _():
        hid_local.start()

    @pl.when((t == 0) & (zq == 0))
    def _():
        hid_remote.start()

    for k in range(4):
        mine = (t == 1) & (zq == 1) & (zr == k)

        @pl.when(mine)
        def _():
            pltpu.make_async_copy(ld.at[k], graw.at[z], gsem.at[z]).start()

        @pl.when(jnp.logical_not(mine))
        def _():
            push(ld.at[k], graw.at[z], ldsend.at[k], gsem.at[z], (4 * t + k, c, 1)).start()

    @pl.when(t == 0)
    def _():
        distribute(z, c, y, zq, zr, push, arrived, sent, cols, wd, qk, wst, qst, wsrc, qsrc, wbuf, qbuf,
                   sibsem, zsend, zsem, psend, psem, rsend, wsem, qsem)

    @pl.when(t == 1)
    def _():
        for k in range(4):
            push(qk.at[4 * k + y], qsrc.at[k], sibsend.at[k], sibsem.at[k], (z, c, 0)).start()
        push(wd, wsrc, sibsend.at[4], sibsem.at[4], (z, c, 0)).start()
        layers(z, c, zq, zr, push, arrived, sent, cols, hid_local, hid_remote, lens, out,
               xbuf, sbuf, nbuf, tbuf, wbuf, qbuf, graw, gbuf, cbuf, mbuf, bits,
               gsem, csend, csem, ssend, ssem, tsend, tsem, nsend, nsem, osend, osem, wsem, qsem)
        for k in range(4):
            sent(qsrc.at[k], sibsend.at[k])
        sent(wsrc, sibsend.at[4])

    @pl.when((t == 0) & (zq == 0))
    def _():
        hid_remote.wait_send()

    for k in range(4):
        mine = (t == 1) & (zq == 1) & (zr == k)

        @pl.when(jnp.logical_not(mine))
        def _():
            sent(ld.at[k], ldsend.at[k])
            arrived(cols(out, k), osem.at[k])


def distribute(z, c, y, zq, zr, push, arrived, sent, cols, wd, qk, wst, qst, wsrc, qsrc, wbuf, qbuf,
               sibsem, zsend, zsem, psend, psem, rsend, wsem, qsem):
    x4 = c - y
    upper, lower = pl.ds(0, HEAD), pl.ds(HEAD, HEAD)

    def scatter():
        for kind in range(2):
            for half in range(2):
                if half and kind == 0:
                    for k in range(4):
                        arrived(qsrc.at[k], sibsem.at[k])
                if half and kind == 1:
                    arrived(wsrc, sibsem.at[4])
                for k in range(4):
                    there = 4 * half + k
                    if kind == 0:
                        src = qsrc.at[k] if half else qk.at[4 * k + y]
                        dst = qst.at[z]
                    else:
                        src = cols(wsrc if half else wd, k)
                        dst = wst.at[z]

                    @pl.when(z != there)
                    def _():
                        push(src, dst, zsend.at[kind, there], zsem.at[kind, z], (there, c, 0)).start()

                    @pl.when(z == there)
                    def _():
                        pltpu.make_async_copy(src, dst, zsem.at[kind, z]).start()

    def staged(kind, l, ref):
        @pl.when(z == l)
        def _():
            pltpu.make_async_copy(ref.at[l], ref.at[l], zsem.at[kind, l]).wait()

        @pl.when(z != l)
        def _():
            arrived(ref.at[l], zsem.at[kind, l])

    @pl.when(z == 0)
    def _():
        scatter()

    def step(l, carry):
        staged(0, l, qst)
        for yy in range(4):
            push(qst.at[l], qbuf.at[l, y], rsend.at[l, 32 + yy], qsem.at[l], (z, x4 + yy, 1)).start()
        staged(1, l, wst)
        for d in range(1, 4):
            push(wst.at[l, upper], wbuf.at[l, c, upper], psend.at[l, 0, d], psem.at[l, 0, c // 4],
                 (z, lax.rem(c + 4 * d, BLOCKS), 0)).start()
            push(wst.at[l, lower], wbuf.at[l, c, lower], psend.at[l, 1, d], psem.at[l, 1, y],
                 (z, x4 + lax.rem(y + d, 4), 0)).start()

        @pl.when((l == 0) & (z > 0))
        def _():
            scatter()

        for d in range(4):
            across = lax.rem(c + 4 * d, BLOCKS)
            along = x4 + lax.rem(y + d, 4)
            if d:
                arrived(wbuf.at[l, across, upper], psem.at[l, 0, across // 4])
                arrived(wbuf.at[l, along, lower], psem.at[l, 1, along - x4])
            for e in (1, 3, 2, 0):
                src = wbuf.at[l, across, upper] if d else wst.at[l, upper]
                push(src, wbuf.at[l, across, upper], rsend.at[l, 4 * d + e], wsem.at[l],
                     (z, x4 + lax.rem(y + e, 4), 1)).start()
                src = wbuf.at[l, along, lower] if d else wst.at[l, lower]
                push(src, wbuf.at[l, along, lower], rsend.at[l, 16 + 4 * d + e], wsem.at[l],
                     (z, lax.rem(c + 4 * e, BLOCKS), 1)).start()
        return carry

    lax.fori_loop(0, LAYERS, step, 0)
    for there in range(LAYERS):

        @pl.when(z != there)
        def _():
            sent(qst.at[z], zsend.at[0, there])
            sent(wst.at[z], zsend.at[1, there])

    def finish(l, carry):
        for e in range(4):
            sent(qst.at[l], rsend.at[l, 32 + e])
            for d in range(1, 4):
                if e < 2:
                    sent(wst.at[l, upper], psend.at[l, e, d])

        def one(e, inner):
            sent(wst.at[l, upper], rsend.at[l, e])
            return inner

        return lax.fori_loop(0, 32, one, carry)

    lax.fori_loop(0, LAYERS, finish, 0)


def layers(z, c, zq, zr, push, arrived, sent, cols, hid_local, hid_remote, lens, out,
           xbuf, sbuf, nbuf, tbuf, wbuf, qbuf, graw, gbuf, cbuf, mbuf, bits,
           gsem, csend, csem, ssend, ssem, tsend, tsem, nsend, nsem, osend, osem, wsem, qsem):
    e1 = lens[0, 0]
    e2 = e1 + lens[0, 1]
    e3 = e2 + lens[0, 2]

    def segment(p):
        return (p >= e1).astype(jnp.int32) + (p >= e2).astype(jnp.int32) + (p >= e3).astype(jnp.int32)

    first = c * ROWS
    seg_row = segment(first + lax.broadcasted_iota(jnp.int32, (ROWS, ROWS), 1))
    seg_col = segment(first + lax.broadcasted_iota(jnp.int32, (ROWS, ROWS), 0))
    later = lax.broadcasted_iota(jnp.int32, (ROWS, ROWS), 0) <= lax.broadcasted_iota(jnp.int32, (ROWS, ROWS), 1)
    small = first + lax.broadcasted_iota(jnp.int32, (8, ROWS), 1)
    seg_small = segment(small)
    seg_last = segment(jnp.full((8, ROWS), first + ROWS - 1, jnp.int32))
    before = jnp.where(c == 0, jnp.full((8, ROWS), -1, jnp.int32), segment(jnp.full((8, ROWS), first - 1, jnp.int32)))
    bits[0] = (seg_small == seg_last).astype(F32)
    bits[1] = (seg_small == before).astype(F32)
    bits[2] = (seg_last == before).astype(F32)
    lane8 = lax.broadcasted_iota(jnp.int32, (8, ROWS), 1)

    for l in range(LAYERS):
        mine = (zq == 1) & (z == l)

        @pl.when(mine)
        def _():
            pltpu.make_async_copy(graw.at[l], graw.at[l], gsem.at[l]).wait()

        @pl.when(jnp.logical_not(mine))
        def _():
            arrived(graw.at[l], gsem.at[l])

    def decays(l, carry):
        g = graw[l]
        for s in (1, 2, 4, 8, 16, 32, 64):
            g = g + jnp.where(lane8 >= s, pltpu.roll(g, s, 1), 0.0)
        gbuf[l] = g
        kept = jnp.exp(jnp.broadcast_to(g[:, ROWS - 1 :], (8, ROWS))) * bits[2]
        cbuf[c, l] = jnp.where(lane8 < HEAD, kept, jnp.broadcast_to(kept[3:4], (8, ROWS)))
        return carry

    lax.fori_loop(0, LAYERS, decays, 0)

    def tell(there, carry):
        push(cbuf.at[c], cbuf.at[c], csend.at[there], csem.at[c], (z, there, 1)).start()
        return carry

    lax.fori_loop(c + 1, BLOCKS, tell, 0)
    allowed = later & (seg_row == seg_col)

    def masks(l, carry):
        for h in range(OWN):
            row = jnp.broadcast_to(gbuf[l, h : h + 1], (ROWS, ROWS))
            mbuf[l, h] = jnp.exp(jnp.where(allowed, row - row.T, -1e30))
        return carry

    lax.fori_loop(0, LAYERS, masks, 0)

    @pl.when(zq == 1)
    def _():
        hid_local.wait()

    @pl.when(zq == 0)
    def _():
        hid_remote.wait_recv()

    def heard(there, carry):
        arrived(cbuf.at[there], csem.at[there])
        return carry

    lax.fori_loop(0, c, heard, 0)
    lane96 = lax.broadcasted_iota(jnp.int32, (HEAD, ROWS), 1)

    def emit(l):
        self_kept = (zq == 1) & (z == l)

        @pl.when(self_kept)
        def _():
            pltpu.make_async_copy(xbuf, cols(out, zr), osem.at[zr]).start()

        @pl.when(jnp.logical_not(self_kept))
        def _():
            push(xbuf, cols(out, zr), osend, osem.at[zr], (l, c, zq)).start()

    def emitted(l):
        self_kept = (zq == 1) & (z == l)

        @pl.when(self_kept)
        def _():
            pltpu.make_async_copy(xbuf, cols(out, zr), osem.at[zr]).wait()

        @pl.when(jnp.logical_not(self_kept))
        def _():
            sent(xbuf, osend)

    def layer(l, carry):
        x = xbuf[...]
        xt = x.astype(F32).T
        own_squares = jnp.sum(xt * xt, axis=0, keepdims=True)
        sbuf[l, z] = own_squares
        for d in (4, 3, 5, 2, 6, 1, 7):
            push(sbuf.at[l, z], sbuf.at[l, z], ssend.at[d], ssem.at[l, z], (lax.rem(z + d, LAYERS), c, 1)).start()
        arrived(qbuf.at[l], qsem.at[l])
        squares = own_squares
        for d in (1, 7, 2, 6, 3, 5, 4):
            there = lax.rem(z + d, LAYERS)
            arrived(sbuf.at[l, there], ssem.at[l, there])
            squares = squares + sbuf[l, there]
        xtb = (xt * lax.rsqrt(squares / MODEL + EPSILON)).astype(BF16)
        raw = [contract(qbuf[l, h], xtb[HEAD * h : HEAD * h + HEAD], 1, 0) for h in range(OWN)]

        @pl.when(l > 0)
        def _():
            emit(l - 1)

        g = gbuf[l]
        key_scale = jnp.exp(jnp.broadcast_to(g[:, ROWS - 1 :], (8, ROWS)) - g) * bits[0]
        query_scale = jnp.exp(g) * bits[1]
        keys, values, keyed = [], [], []
        for h in range(OWN):
            k = jax.nn.silu(raw[h][HEAD : 2 * HEAD]).astype(BF16)
            keys.append(k)
            values.append(raw[h][2 * HEAD :].astype(BF16))
            keyed.append((k.astype(F32) * key_scale[h : h + 1]).astype(BF16))
        for p in range(3):
            right = jnp.concatenate([keyed[p], keyed[3][32 * p : 32 * p + 32]], axis=0)
            both = contract(jnp.concatenate([values[p], values[3]], axis=0), right, 1, 1)
            tbuf[l, c, HEAD * p : HEAD * p + HEAD] = jnp.where(lane96 < HEAD, both[:HEAD], both[HEAD:]).astype(BF16)

        def states_out(there, carry):
            push(tbuf.at[l, c], tbuf.at[l, c], tsend.at[there], tsem.at[l, c], (z, there, 1)).start()
            return carry

        lax.fori_loop(c + 1, BLOCKS, states_out, 0)

        inner, queried = [], []
        for h in range(OWN):
            q = jax.nn.silu(raw[h][:HEAD]).astype(BF16)
            scores = contract(keys[h], q, 0, 0)
            weights = (scores * mbuf[l, h]).astype(BF16)
            inner.append(contract(values[h], weights, 1, 0))
            queried.append((q.astype(F32) * query_scale[h : h + 1]).astype(BF16))

        def fold(there, state):
            arrived(tbuf.at[l, there], tsem.at[l, there])
            return tuple(
                s * cbuf[there, l, p : p + 1] + tbuf[l, there, HEAD * p : HEAD * p + HEAD].astype(F32)
                for p, s in enumerate(state)
            )

        state = lax.fori_loop(0, c, fold, tuple(jnp.zeros((HEAD, ROWS), F32) for _ in range(3)))
        attended = list(inner)
        for p in range(3):
            left = jnp.concatenate([queried[p], jnp.zeros((32, ROWS), BF16)], axis=0)
            right = jnp.concatenate([jnp.zeros((HEAD, ROWS), BF16), queried[3][32 * p : 32 * p + 32]], axis=0)
            both = contract(state[p].astype(BF16), jnp.concatenate([left, right], axis=1), 1, 0)
            attended[p] = attended[p] + both[:, :ROWS]
            attended[3] = attended[3] + both[:, ROWS:]
        normed = [a * lax.rsqrt(jnp.mean(a * a, axis=0, keepdims=True) + EPSILON) for a in attended]
        nbuf[l, z] = jnp.concatenate(normed, axis=0).T.astype(BF16)
        def onward(source, rows, slot, d):
            part = nbuf.at[l, source, rows]
            return push(part, part, nsend.at[slot], nsem.at[l, source], (lax.rem(z + d, LAYERS), c, 1))

        every, early, late = pl.ds(0, ROWS), pl.ds(0, ROWS // 2), pl.ds(ROWS // 2, ROWS // 2)
        behind, ahead = lax.rem(z + 6, LAYERS), lax.rem(z + 2, LAYERS)
        copies = [onward(z, every, slot, d) for slot, d in enumerate((2, 6, 1, 7))]
        for copy in copies:
            copy.start()

        def project(total, d):
            there = lax.rem(z + d, LAYERS)
            weight = wbuf[l, pl.ds(2 * there, 2)].reshape(WIDE, WIDE)
            return total + contract(nbuf[l, there], weight, 1, 0)

        def gathered(d):
            there = lax.rem(z + d, LAYERS)
            arrived(nbuf.at[l, there], nsem.at[l, there])

        arrived(wbuf.at[l], wsem.at[l])
        total = project(x.astype(F32), 0)
        for d, source, rows, one, two in ((6, behind, early, 1, 2), (2, ahead, late, 7, 6)):
            gathered(d)
            far = [onward(source, rows, len(copies), two), onward(source, every, len(copies) + 1, one)]
            for copy in far:
                copy.start()
            copies += far
        for d in (1, 7, 2, 6, 3, 5, 4):
            if d not in (2, 6):
                gathered(d)
            total = project(total, d)

        @pl.when(l > 0)
        def _():
            emitted(l - 1)

        xbuf[...] = total.astype(BF16)
        for d in range(1, LAYERS):
            sent(sbuf.at[l, z], ssend.at[d])
        for copy in copies:
            copy.wait_send()

        def states_sent(there, carry):
            sent(tbuf.at[l, c], tsend.at[there])
            return carry

        lax.fori_loop(c + 1, BLOCKS, states_sent, 0)
        return carry

    lax.fori_loop(0, LAYERS, layer, 0)
    emit(LAYERS - 1)
    emitted(LAYERS - 1)

    def told(there, carry):
        sent(cbuf.at[c], csend.at[there])
        return carry

    lax.fori_loop(c + 1, BLOCKS, told, 0)


def shards(hidden_in, qkv_weight, log_decay, lengths, out_mantissa, out_exponent):
    ctx = lax.axis_index("ctx")
    exponent = lax.dynamic_slice_in_dim(out_exponent[0], 2 * ctx, 2, 0)
    scale = jnp.exp2(exponent.astype(F32))
    scale = jnp.repeat(scale, HEAD, axis=1)[:, None, :]
    weight = (out_mantissa[0].astype(F32).reshape(2, HEAD, -1) * scale).reshape(2 * HEAD, -1).astype(BF16)
    qkv = qkv_weight[0].swapaxes(1, 2)
    decay = jnp.pad(log_decay[0, 0].T.reshape(4, OWN, ROWS), ((0, 0), (0, 8 - OWN), (0, 0)))
    half = hidden_in.shape[2]
    dma = pltpu.SemaphoreType.DMA
    anywhere = pl.BlockSpec(memory_space=pl.ANY)
    outputs = pl.pallas_call(
        kernel,
        out_shape=jax.ShapeDtypeStruct((ROWS, half), BF16),
        in_specs=[anywhere] * 4 + [pl.BlockSpec(memory_space=pltpu.SMEM)],
        out_specs=anywhere,
        scratch_shapes=[
            pltpu.VMEM((ROWS, WIDE), BF16),
            pltpu.VMEM((LAYERS, LAYERS, 1, ROWS), F32),
            pltpu.VMEM((LAYERS, LAYERS, ROWS, WIDE), BF16),
            pltpu.VMEM((LAYERS, BLOCKS, 3 * HEAD, ROWS), BF16),
            pltpu.VMEM((LAYERS, BLOCKS, 2 * HEAD, WIDE), BF16),
            pltpu.VMEM((LAYERS, OWN, 3 * HEAD, HEAD), BF16),
            pltpu.VMEM((LAYERS, 8, ROWS), F32),
            pltpu.VMEM((LAYERS, 8, ROWS), F32),
            pltpu.VMEM((BLOCKS, LAYERS, 8, ROWS), F32),
            pltpu.VMEM((LAYERS, OWN, ROWS, ROWS), F32),
            pltpu.VMEM((LAYERS, 2 * HEAD, WIDE), BF16),
            pltpu.VMEM((LAYERS, 3 * HEAD, HEAD), BF16),
            pltpu.VMEM((2 * HEAD, half), BF16),
            pltpu.VMEM((4, 3 * HEAD, HEAD), BF16),
            pltpu.VMEM((3, 8, ROWS), F32),
            dma((4,)),
            dma,
            dma((7,)),
            dma((5,)),
            dma((LAYERS,)),
            dma((BLOCKS,)),
            dma((BLOCKS,)),
            dma((LAYERS,)),
            dma((LAYERS, LAYERS)),
            dma((BLOCKS,)),
            dma((LAYERS, BLOCKS)),
            dma((LAYERS,)),
            dma((LAYERS, LAYERS)),
            dma,
            dma((4,)),
            dma((2, LAYERS)),
            dma((2, LAYERS)),
            dma((LAYERS, 2, 4)),
            dma((LAYERS, 2, 4)),
            dma((LAYERS, 36)),
            dma((LAYERS,)),
            dma((LAYERS,)),
        ],
        compiler_params=pltpu.CompilerParams(collective_id=0, has_side_effects=True, vmem_limit_bytes=58 << 20),
    )(hidden_in[0], weight, qkv, decay, lengths)
    return outputs[None, None]


def solution(mesh):
    in_specs = (
        P(None, "ctx", "tp"),
        P("phase", "tp", None, None),
        P("phase", None, "ctx", "tp"),
        P(),
        P("phase", "ctx", "tp"),
        P("phase", None, "tp"),
    )
    out_specs = P("phase", None, "ctx", "tp")
    return jax.shard_map(shards, mesh=mesh, in_specs=in_specs, out_specs=out_specs, check_vma=False)
```

```python
import jax
import jax.numpy as jnp
from jax import lax
from jax.experimental import pallas as pl
from jax.experimental.pallas import tpu as pltpu
from jax.sharding import PartitionSpec as P

EPSILON = 1e-05
MESH = pl.DeviceIdType.MESH
LAYERS = 8
BLOCKS = 16
ROWS = 128
HEAD = 96
OWN = 4
WIDE = OWN * HEAD
MODEL = 3072
F32 = jnp.float32
BF16 = jnp.bfloat16


def contract(a, b, da, db):
    return lax.dot_general(a, b, (((da,), (db,)), ((), ())), preferred_element_type=F32)


def kernel(
    hid, qkv, decay, lens, mantissa, exponent, out,
    xbuf, sbuf, nbuf, tbuf, wbuf, qbuf, graw, gbuf, cbuf, mbuf, allow, wst, qst, wsrc, qsrc,
    bits, ldsend, hsem, sibsend, sibsem, gsem, csend, csem,
    ssend, ssem, tsend, tsem, nsend, nsem, osend, osem,
    zsend, zsem, psend, psem, rsend, wsem, qsem, nsem2,
    wd, qk, ld, mraw, qraw, draw, eraw, loadsem,
):
    z, c, t = lax.axis_index("phase"), lax.axis_index("ctx"), lax.axis_index("tp")
    y = lax.rem(c, 4)
    zq, zr = z // 4, lax.rem(z, 4)

    def push(src, dst, s, r, dev):
        return pltpu.make_async_remote_copy(
            src_ref=src, dst_ref=dst, send_sem=s, recv_sem=r, device_id=dev, device_id_type=MESH
        )

    def arrived(dst, r):
        push(dst, dst, r, r, (z, c, 1 - t)).wait_recv()

    def sent(src, s):
        push(src, src, s, s, (z, c, 1 - t)).wait_send()

    def cols(ref, k):
        return ref.at[:, pl.ds(pl.multiple_of(WIDE * k, 128), WIDE)]

    barrier = pltpu.get_barrier_semaphore()

    def greet(dev):
        pl.semaphore_signal(barrier, inc=1, device_id=dev, device_id_type=MESH)

    greet((z, c, 1 - t))
    for d in range(1, LAYERS):
        for core in range(2):
            greet((lax.rem(z + d, LAYERS), c, core))

    def greet_plane(d, carry):
        for core in range(2):
            greet((z, lax.rem(c + d, BLOCKS), core))
        return carry

    lax.fori_loop(1, BLOCKS, greet_plane, 0)

    loads = [pltpu.make_async_copy(qkv.at[4 * k + y], qraw.at[k], loadsem.at[k]) for k in range(4)]
    loads += [
        pltpu.make_async_copy(mantissa, mraw, loadsem.at[4]),
        pltpu.make_async_copy(decay, draw, loadsem.at[5]),
        pltpu.make_async_copy(exponent, eraw, loadsem.at[6]),
    ]
    for load in loads:
        load.start()
    for k in range(4):
        loads[k].wait()
        qk[k] = qraw[k].astype(F32).T.astype(BF16)
    loads[5].wait()
    flipped = draw[...]
    for k in range(4):
        ld[k] = jnp.concatenate([flipped[OWN * k : OWN * k + OWN], jnp.zeros((8 - OWN, ROWS), F32)], axis=0)
    loads[6].wait()
    loads[4].wait()
    power = eraw[...]
    scale = jnp.full(power.shape, 2.0, F32)
    for value in range(4):
        scale = jnp.where(power == value - 3, 2.0 ** (value - 3), scale)
    spots = (4 * OWN, MODEL // 2)
    inside = lax.broadcasted_iota(jnp.int32, spots, 1) - HEAD * lax.broadcasted_iota(jnp.int32, spots, 0)
    spread = ((inside >= 0) & (inside < HEAD)).astype(BF16)
    scale = contract(scale.astype(BF16), spread, 0, 0)
    here = lax.broadcasted_iota(jnp.int32, scale.shape, 0) - 2 * c
    scale = [jnp.sum(jnp.where(here == r, scale, 0.0), axis=0, keepdims=True) for r in range(2)]
    for r in range(2):
        part = mraw[HEAD * r : HEAD * r + HEAD].astype(F32) * scale[r]
        wd[HEAD * r : HEAD * r + HEAD] = part.astype(BF16)
    pl.semaphore_wait(barrier, 2 * (LAYERS + BLOCKS) - 3)

    hid_local = pltpu.make_async_copy(cols(hid, zr), xbuf.at[0], hsem)
    hid_remote = push(cols(hid, zr), xbuf.at[0], sibsend.at[2], hsem, (z, c, 1))

    @pl.when((t == 1) & (zq == 1))
    def _():
        hid_local.start()

    @pl.when((t == 0) & (zq == 0))
    def _():
        hid_remote.start()

    for k in range(4):
        mine = (t == 1) & (zq == 1) & (zr == k)

        @pl.when(mine)
        def _():
            pltpu.make_async_copy(ld.at[k], graw.at[z], gsem.at[z]).start()

        @pl.when(jnp.logical_not(mine))
        def _():
            push(ld.at[k], graw.at[z], ldsend.at[k], gsem.at[z], (4 * t + k, c, 1)).start()

    @pl.when(t == 0)
    def _():
        distribute(z, c, y, zq, zr, push, arrived, sent, cols, wd, qk, wst, qst, wsrc, qsrc, wbuf, qbuf,
                   sibsem, zsend, zsem, psend, psem, rsend, wsem, qsem)

    @pl.when(t == 1)
    def _():
        @pl.when(z == 0)
        def _():
            for k in range(4):
                push(qk.at[k], qst.at[0], zsend.at[0, 4 + k], zsem.at[0, 0], (4 + k, c, 0)).start()
            for k in range(4):
                push(cols(wd, k), wst.at[0], zsend.at[1, 4 + k], zsem.at[1, 0], (4 + k, c, 0)).start()

        @pl.when(z > 0)
        def _():
            push(qk, qsrc, sibsend.at[0], sibsem.at[0], (z, c, 0)).start()
            push(wd, wsrc, sibsend.at[1], sibsem.at[1], (z, c, 0)).start()

        layers(z, c, zq, zr, push, arrived, sent, cols, hid_local, hid_remote, lens, out,
               xbuf, sbuf, nbuf, tbuf, wbuf, qbuf, graw, gbuf, cbuf, mbuf, allow, bits,
               gsem, csend, csem, ssend, ssem, tsend, tsem, nsend, nsem, osend, osem, wsem, qsem, nsem2)

        @pl.when(z == 0)
        def _():
            for k in range(4):
                sent(qk.at[k], zsend.at[0, 4 + k])
                sent(cols(wd, k), zsend.at[1, 4 + k])

        @pl.when(z > 0)
        def _():
            sent(qsrc, sibsend.at[0])
            sent(wsrc, sibsend.at[1])

    @pl.when((t == 0) & (zq == 0))
    def _():
        hid_remote.wait_send()

    for k in range(4):
        mine = (t == 1) & (zq == 1) & (zr == k)

        @pl.when(jnp.logical_not(mine))
        def _():
            sent(ld.at[k], ldsend.at[k])
            arrived(cols(out, k), osem.at[k])


def distribute(z, c, y, zq, zr, push, arrived, sent, cols, wd, qk, wst, qst, wsrc, qsrc, wbuf, qbuf,
               sibsem, zsend, zsem, psend, psem, rsend, wsem, qsem):
    x4 = c - y
    upper, lower = pl.ds(0, HEAD), pl.ds(HEAD, HEAD)

    def scatter(halves):
        for kind in range(2):
            for half in halves:
                if half:
                    arrived(wsrc if kind else qsrc, sibsem.at[kind])
                for k in range(4):
                    there = 4 * half + k
                    if kind == 0:
                        src = qsrc.at[k] if half else qk.at[k]
                        dst = qst.at[z]
                    else:
                        src = cols(wsrc if half else wd, k)
                        dst = wst.at[z]

                    @pl.when(z != there)
                    def _():
                        push(src, dst, zsend.at[kind, there], zsem.at[kind, z], (there, c, 0)).start()

                    @pl.when(z == there)
                    def _():
                        pltpu.make_async_copy(src, dst, zsem.at[kind, z]).start()

    def staged(kind, l, ref):
        @pl.when(z == l)
        def _():
            pltpu.make_async_copy(ref.at[l], ref.at[l], zsem.at[kind, l]).wait()

        @pl.when(z != l)
        def _():
            arrived(ref.at[l], zsem.at[kind, l])

    @pl.when(z == 0)
    def _():
        scatter((0,))

    def first_hop(l):
        staged(0, l, qst)
        for yy in range(4):
            push(qst.at[l], qbuf.at[l, y], rsend.at[l, 32 + yy], qsem.at[l], (z, x4 + yy, 1)).start()
        staged(1, l, wst)
        for d in range(1, 4):
            push(wst.at[l, upper], wbuf.at[l, c, upper], psend.at[l, 0, d], psem.at[l, 0, c // 4],
                 (z, lax.rem(c + 4 * d, BLOCKS), 0)).start()
            push(wst.at[l, lower], wbuf.at[l, c, lower], psend.at[l, 1, d], psem.at[l, 1, y],
                 (z, x4 + lax.rem(y + d, 4), 0)).start()

    def second_hop(l):
        for d in range(4):
            across = lax.rem(c + 4 * d, BLOCKS)
            along = x4 + lax.rem(y + d, 4)
            if d:
                arrived(wbuf.at[l, across, upper], psem.at[l, 0, across // 4])
                arrived(wbuf.at[l, along, lower], psem.at[l, 1, along - x4])
            for e in (1, 3, 2, 0):
                src = wbuf.at[l, across, upper] if d else wst.at[l, upper]
                push(src, wbuf.at[l, across, upper], rsend.at[l, 4 * d + e], wsem.at[l],
                     (z, x4 + lax.rem(y + e, 4), 1)).start()
                src = wbuf.at[l, along, lower] if d else wst.at[l, lower]
                push(src, wbuf.at[l, along, lower], rsend.at[l, 16 + 4 * d + e], wsem.at[l],
                     (z, lax.rem(c + 4 * e, BLOCKS), 1)).start()

    def step(l, carry):
        second_hop(l)

        @pl.when(l < LAYERS - 1)
        def _():
            first_hop(l + 1)

        return carry

    @pl.when(z > 0)
    def _():
        scatter((0, 1))

    first_hop(0)

    lax.fori_loop(0, LAYERS, step, 0)
    for there in range(LAYERS):

        @pl.when((z != there) & (z > 0) if there >= 4 else z != there)
        def _():
            sent(qst.at[z], zsend.at[0, there])
            sent(wst.at[z], zsend.at[1, there])

    def finish(l, carry):
        for e in range(4):
            sent(qst.at[l], rsend.at[l, 32 + e])
            for d in range(1, 4):
                if e < 2:
                    sent(wst.at[l, upper], psend.at[l, e, d])

        def one(e, inner):
            sent(wst.at[l, upper], rsend.at[l, e])
            return inner

        return lax.fori_loop(0, 32, one, carry)

    lax.fori_loop(0, LAYERS, finish, 0)


def layers(z, c, zq, zr, push, arrived, sent, cols, hid_local, hid_remote, lens, out,
           xbuf, sbuf, nbuf, tbuf, wbuf, qbuf, graw, gbuf, cbuf, mbuf, allow, bits,
           gsem, csend, csem, ssend, ssem, tsend, tsem, nsend, nsem, osend, osem, wsem, qsem, nsem2):
    e1 = lens[0, 0]
    e2 = e1 + lens[0, 1]
    e3 = e2 + lens[0, 2]

    def segment(p):
        return (p >= e1).astype(jnp.int32) + (p >= e2).astype(jnp.int32) + (p >= e3).astype(jnp.int32)

    first = c * ROWS
    seg_row = segment(first + lax.broadcasted_iota(jnp.int32, (ROWS, ROWS), 1))
    seg_col = segment(first + lax.broadcasted_iota(jnp.int32, (ROWS, ROWS), 0))
    later = lax.broadcasted_iota(jnp.int32, (ROWS, ROWS), 0) <= lax.broadcasted_iota(jnp.int32, (ROWS, ROWS), 1)
    small = first + lax.broadcasted_iota(jnp.int32, (8, ROWS), 1)
    seg_small = segment(small)
    seg_last = segment(jnp.full((8, ROWS), first + ROWS - 1, jnp.int32))
    before = jnp.where(c == 0, jnp.full((8, ROWS), -1, jnp.int32), segment(jnp.full((8, ROWS), first - 1, jnp.int32)))
    bits[0] = (seg_small == seg_last).astype(F32)
    bits[1] = (seg_small == before).astype(F32)
    bits[2] = (seg_last == before).astype(F32)
    lane8 = lax.broadcasted_iota(jnp.int32, (8, ROWS), 1)

    for l in range(LAYERS):
        mine = (zq == 1) & (z == l)

        @pl.when(mine)
        def _():
            pltpu.make_async_copy(graw.at[l], graw.at[l], gsem.at[l]).wait()

        @pl.when(jnp.logical_not(mine))
        def _():
            arrived(graw.at[l], gsem.at[l])

    g = graw[...].reshape(LAYERS * 8, ROWS)
    lane = lax.broadcasted_iota(jnp.int32, (LAYERS * 8, ROWS), 1)
    for s in (1, 2, 4, 8, 16, 32, 64):
        g = g + jnp.where(lane >= s, pltpu.roll(g, s, 1), 0.0)
    gbuf[...] = g.reshape(LAYERS, 8, ROWS)
    for l in range(LAYERS):
        kept = jnp.exp(jnp.broadcast_to(g[8 * l : 8 * l + 8, ROWS - 1 :], (8, ROWS))) * bits[2]
        cbuf[c, l] = jnp.where(lane8 < HEAD, kept, jnp.broadcast_to(kept[3:4], (8, ROWS)))

    def tell(there, carry):
        push(cbuf.at[c], cbuf.at[c], csend.at[there], csem.at[c], (z, there, 1)).start()
        return carry

    lax.fori_loop(c + 1, BLOCKS, tell, 0)
    allow[...] = jnp.where(later & (seg_row == seg_col), 0.0, -1e30)

    @pl.when(zq == 1)
    def _():
        hid_local.wait()

    @pl.when(zq == 0)
    def _():
        hid_remote.wait_recv()

    lane96 = lax.broadcasted_iota(jnp.int32, (HEAD, ROWS), 1)

    def emit(l):
        self_kept = (zq == 1) & (z == l)

        @pl.when(self_kept)
        def _():
            pltpu.make_async_copy(xbuf.at[l + 1], cols(out, zr), osem.at[zr]).start()

        @pl.when(jnp.logical_not(self_kept))
        def _():
            push(xbuf.at[l + 1], cols(out, zr), osend.at[l], osem.at[zr], (l, c, zq)).start()

    def emitted(l):
        self_kept = (zq == 1) & (z == l)

        @pl.when(self_kept)
        def _():
            pltpu.make_async_copy(xbuf.at[l + 1], cols(out, zr), osem.at[zr]).wait()

        @pl.when(jnp.logical_not(self_kept))
        def _():
            sent(xbuf.at[l + 1], osend.at[l])

    def gone(l):
        for slot in range(10):
            if slot in (4, 5, 8, 9):
                sent(nbuf.at[l, z], nsend.at[l, slot])
            else:
                sent(nbuf.at[l, z, pl.ds(0, ROWS // 2)], nsend.at[l, slot])

    def layer(l, carry):
        x = xbuf[l]
        xt = x.astype(F32).T
        own_squares = jnp.sum(xt * xt, axis=0, keepdims=True)
        sbuf[l, z] = own_squares
        for d in (4, 3, 5, 2, 6, 1, 7):
            push(sbuf.at[l, z], sbuf.at[l, z], ssend.at[l, d], ssem.at[l, z], (lax.rem(z + d, LAYERS), c, 1)).start()
        for h in range(OWN):
            row = jnp.broadcast_to(gbuf[l, h : h + 1], (ROWS, ROWS))
            mbuf[h] = jnp.exp(row - row.T + allow[...])

        @pl.when(l > 0)
        def _():
            gone(l - 1)

        arrived(qbuf.at[l], qsem.at[l])
        squares = own_squares
        for d in (1, 7, 2, 6, 3, 5, 4):
            there = lax.rem(z + d, LAYERS)
            arrived(sbuf.at[l, there], ssem.at[l, there])
            squares = squares + sbuf[l, there]
        xtb = (xt * lax.rsqrt(squares / MODEL + EPSILON)).astype(BF16)
        heads = [xtb[HEAD * h : HEAD * h + HEAD] for h in range(OWN)]
        raw = [contract(qbuf[l, h, HEAD:], heads[h], 1, 0) for h in range(OWN)]

        @pl.when(l > 0)
        def _():
            emit(l - 1)

        g = gbuf[l]
        key_scale = jnp.exp(jnp.broadcast_to(g[:, ROWS - 1 :], (8, ROWS)) - g) * bits[0]
        query_scale = jnp.exp(g) * bits[1]
        keys, values, keyed = [], [], []
        for h in range(OWN):
            k = jax.nn.silu(raw[h][:HEAD]).astype(BF16)
            keys.append(k)
            values.append(raw[h][HEAD:].astype(BF16))
            keyed.append((k.astype(F32) * key_scale[h : h + 1]).astype(BF16))
        for p in range(3):
            right = jnp.concatenate([keyed[p], keyed[3][32 * p : 32 * p + 32]], axis=0)
            both = contract(jnp.concatenate([values[p], values[3]], axis=0), right, 1, 1)
            tbuf[l, c, HEAD * p : HEAD * p + HEAD] = jnp.where(lane96 < HEAD, both[:HEAD], both[HEAD:]).astype(BF16)

        def states_out(there, carry):
            push(tbuf.at[l, c], tbuf.at[l, c], tsend.at[l, there], tsem.at[l, c], (z, there, 1)).start()
            return carry

        lax.fori_loop(c + 1, BLOCKS, states_out, 0)

        inner, queried = [], []
        for h in range(OWN):
            q = jax.nn.silu(contract(qbuf[l, h, :HEAD], heads[h], 1, 0)).astype(BF16)
            scores = contract(keys[h], q, 0, 0)
            weights = (scores * mbuf[h]).astype(BF16)
            inner.append(contract(values[h], weights, 1, 0))
            queried.append((q.astype(F32) * query_scale[h : h + 1]).astype(BF16))

        def fold(there, state):
            @pl.when(l == 0)
            def _():
                arrived(cbuf.at[there], csem.at[there])

            arrived(tbuf.at[l, there], tsem.at[l, there])
            return tuple(
                s * cbuf[there, l, p : p + 1] + tbuf[l, there, HEAD * p : HEAD * p + HEAD].astype(F32)
                for p, s in enumerate(state)
            )

        state = lax.fori_loop(0, c, fold, tuple(jnp.zeros((HEAD, ROWS), F32) for _ in range(3)))

        attended = list(inner)
        for p in range(3):
            left = jnp.concatenate([queried[p], jnp.zeros((32, ROWS), BF16)], axis=0)
            right = jnp.concatenate([jnp.zeros((HEAD, ROWS), BF16), queried[3][32 * p : 32 * p + 32]], axis=0)
            both = contract(state[p].astype(BF16), jnp.concatenate([left, right], axis=1), 1, 0)
            attended[p] = attended[p] + both[:, :ROWS]
            attended[3] = attended[3] + both[:, ROWS:]
        normed = [a * lax.rsqrt(jnp.mean(a * a, axis=0, keepdims=True) + EPSILON) for a in attended]
        nbuf[l, z] = jnp.concatenate(normed, axis=0).T.astype(BF16)
        def onward(source, rows, slot, d, sem=nsem):
            part = nbuf.at[l, source, rows]
            return push(part, part, nsend.at[l, slot], sem.at[l, source], (lax.rem(z + d, LAYERS), c, 1))

        every, early, late = pl.ds(0, ROWS), pl.ds(0, ROWS // 2), pl.ds(ROWS // 2, ROWS // 2)
        behind, ahead = lax.rem(z + 6, LAYERS), lax.rem(z + 2, LAYERS)
        onward(z, early, 0, 2).start()
        onward(z, late, 1, 6).start()
        onward(z, late, 2, 2, nsem2).start()
        onward(z, early, 3, 6, nsem2).start()
        onward(z, every, 4, 1).start()
        onward(z, every, 5, 7).start()

        def project(total, d):
            there = lax.rem(z + d, LAYERS)
            weight = wbuf[l, pl.ds(2 * there, 2)].reshape(WIDE, WIDE)
            return total + contract(nbuf[l, there], weight, 1, 0)

        def gathered(d):
            there = lax.rem(z + d, LAYERS)
            arrived(nbuf.at[l, there], nsem.at[l, there])

        for d in range(1, LAYERS):
            sent(sbuf.at[l, z], ssend.at[l, d])

        def states_sent(there, inner):
            sent(tbuf.at[l, c], tsend.at[l, there])
            return inner

        lax.fori_loop(c + 1, BLOCKS, states_sent, 0)
        arrived(wbuf.at[l], wsem.at[l])
        total = project(x.astype(F32), 0)
        for source, rows, slot, two in ((behind, early, 6, 2), (ahead, late, 7, 6)):
            arrived(nbuf.at[l, source, rows], nsem.at[l, source])
            onward(source, rows, slot, two).start()
        for source, rows, slot, one in ((behind, late, 8, 1), (ahead, early, 9, 7)):
            arrived(nbuf.at[l, source, rows], nsem2.at[l, source])
            onward(source, every, slot, one).start()
        for d in (1, 7, 2, 6, 3, 5, 4):
            if d not in (2, 6):
                gathered(d)
            total = project(total, d)

        xbuf[l + 1] = total.astype(BF16)
        return carry

    lax.fori_loop(0, LAYERS, layer, 0)
    emit(LAYERS - 1)

    gone(LAYERS - 1)

    def settle(l, carry):
        emitted(l)
        return carry

    lax.fori_loop(0, LAYERS, settle, 0)

    def told(there, carry):
        sent(cbuf.at[c], csend.at[there])
        return carry

    lax.fori_loop(c + 1, BLOCKS, told, 0)


def shards(hidden_in, qkv_weight, log_decay, lengths, out_mantissa, out_exponent):
    half = hidden_in.shape[2]
    dma = pltpu.SemaphoreType.DMA
    anywhere = pl.BlockSpec(memory_space=pl.ANY)
    outputs = pl.pallas_call(
        kernel,
        out_shape=jax.ShapeDtypeStruct((ROWS, half), BF16),
        in_specs=[anywhere] * 3 + [pl.BlockSpec(memory_space=pltpu.SMEM)] + [anywhere] * 2,
        out_specs=anywhere,
        scratch_shapes=[
            pltpu.VMEM((LAYERS + 1, ROWS, WIDE), BF16),
            pltpu.VMEM((LAYERS, LAYERS, 1, ROWS), F32),
            pltpu.VMEM((LAYERS, LAYERS, ROWS, WIDE), BF16),
            pltpu.VMEM((LAYERS, BLOCKS, 3 * HEAD, ROWS), BF16),
            pltpu.VMEM((LAYERS, BLOCKS, 2 * HEAD, WIDE), BF16),
            pltpu.VMEM((LAYERS, OWN, 3 * HEAD, HEAD), BF16),
            pltpu.VMEM((LAYERS, 8, ROWS), F32),
            pltpu.VMEM((LAYERS, 8, ROWS), F32),
            pltpu.VMEM((BLOCKS, LAYERS, 8, ROWS), F32),
            pltpu.VMEM((OWN, ROWS, ROWS), F32),
            pltpu.VMEM((ROWS, ROWS), F32),
            pltpu.VMEM((LAYERS, 2 * HEAD, WIDE), BF16),
            pltpu.VMEM((LAYERS, 3 * HEAD, HEAD), BF16),
            pltpu.VMEM((2 * HEAD, half), BF16),
            pltpu.VMEM((4, 3 * HEAD, HEAD), BF16),
            pltpu.VMEM((3, 8, ROWS), F32),
            dma((4,)),
            dma,
            dma((3,)),
            dma((2,)),
            dma((LAYERS,)),
            dma((BLOCKS,)),
            dma((BLOCKS,)),
            dma((LAYERS, LAYERS)),
            dma((LAYERS, LAYERS)),
            dma((LAYERS, BLOCKS)),
            dma((LAYERS, BLOCKS)),
            dma((LAYERS, 10)),
            dma((LAYERS, LAYERS)),
            dma((LAYERS,)),
            dma((4,)),
            dma((2, LAYERS)),
            dma((2, LAYERS)),
            dma((LAYERS, 2, 4)),
            dma((LAYERS, 2, 4)),
            dma((LAYERS, 36)),
            dma((LAYERS,)),
            dma((LAYERS,)),
            dma((LAYERS, LAYERS)),
            pltpu.VMEM((2 * HEAD, half), BF16),
            pltpu.VMEM((4, 3 * HEAD, HEAD), BF16),
            pltpu.VMEM((4, 8, ROWS), F32),
            pltpu.VMEM((2 * HEAD, half), BF16),
            pltpu.VMEM((4, HEAD, 3 * HEAD), BF16),
            pltpu.VMEM((4 * OWN, ROWS), F32),
            pltpu.VMEM((4 * OWN, 2 * OWN * 4), jnp.int32),
            dma((7,)),
        ],
        compiler_params=pltpu.CompilerParams(collective_id=0, has_side_effects=True, vmem_limit_bytes=58 << 20),
    )(hidden_in[0], qkv_weight[0], log_decay[0, 0].T, lengths, out_mantissa[0], out_exponent[0].T)
    return outputs[None, None]


def solution(mesh):
    in_specs = (
        P(None, "ctx", "tp"),
        P("phase", "tp", None, None),
        P("phase", None, "ctx", "tp"),
        P(),
        P("phase", "ctx", "tp"),
        P("phase", None, "tp"),
    )
    out_specs = P("phase", None, "ctx", "tp")
    return jax.shard_map(shards, mesh=mesh, in_specs=in_specs, out_specs=out_specs, check_vma=False)
```

```python
import jax
import jax.numpy as jnp
from jax import lax
from jax.experimental import pallas as pl
from jax.experimental.pallas import tpu as pltpu
from jax.sharding import PartitionSpec as P

EPSILON = 1e-05
MESH = pl.DeviceIdType.MESH
LAYERS = 8
BLOCKS = 16
ROWS = 128
HEAD = 96
OWN = 4
WIDE = OWN * HEAD
MODEL = 3072
F32 = jnp.float32
BF16 = jnp.bfloat16


def contract(a, b, da, db):
    return lax.dot_general(a, b, (((da,), (db,)), ((), ())), preferred_element_type=F32)


def kernel(
    hid, qkv, decay, lens, mantissa, exponent, out,
    xbuf, sbuf, nbuf, tbuf, wbuf, qbuf, graw, gbuf, cbuf, mbuf, allow, wst, qst, wsrc, qsrc,
    bits, ldsend, hsem, sibsend, sibsem, gsem, csend, csem,
    ssend, ssem, tsend, tsem, nsend, nsem, osend, osem,
    zsend, zsem, psend, psem, rsend, wsem, qsem, nsem2,
    wd, qk, ld, mraw, qraw, draw, eraw, loadsem,
):
    z, c, t = lax.axis_index("phase"), lax.axis_index("ctx"), lax.axis_index("tp")
    y = lax.rem(c, 4)
    zq, zr = z // 4, lax.rem(z, 4)

    def push(src, dst, s, r, dev):
        return pltpu.make_async_remote_copy(
            src_ref=src, dst_ref=dst, send_sem=s, recv_sem=r, device_id=dev, device_id_type=MESH
        )

    def arrived(dst, r):
        push(dst, dst, r, r, (z, c, 1 - t)).wait_recv()

    def sent(src, s):
        push(src, src, s, s, (z, c, 1 - t)).wait_send()

    def cols(ref, k):
        return ref.at[:, pl.ds(pl.multiple_of(WIDE * k, 128), WIDE)]

    barrier = pltpu.get_barrier_semaphore()

    def greet(dev):
        pl.semaphore_signal(barrier, inc=1, device_id=dev, device_id_type=MESH)

    greet((z, c, 1 - t))
    for d in range(1, LAYERS):
        for core in range(2):
            greet((lax.rem(z + d, LAYERS), c, core))

    def greet_plane(d, carry):
        for core in range(2):
            greet((z, lax.rem(c + d, BLOCKS), core))
        return carry

    lax.fori_loop(1, BLOCKS, greet_plane, 0)

    loads = [pltpu.make_async_copy(qkv.at[4 * k + y], qraw.at[k], loadsem.at[k]) for k in range(4)]
    loads += [
        pltpu.make_async_copy(mantissa, mraw, loadsem.at[4]),
        pltpu.make_async_copy(decay, draw, loadsem.at[5]),
        pltpu.make_async_copy(exponent, eraw, loadsem.at[6]),
    ]
    for load in loads:
        load.start()
    for k in range(4):
        loads[k].wait()
        qk[k] = qraw[k].astype(F32).T.astype(BF16)
    loads[5].wait()
    flipped = draw[...]
    for k in range(4):
        ld[k] = jnp.concatenate([flipped[OWN * k : OWN * k + OWN], jnp.zeros((8 - OWN, ROWS), F32)], axis=0)
    loads[6].wait()
    loads[4].wait()
    power = eraw[...]
    scale = jnp.full(power.shape, 2.0, F32)
    for value in range(4):
        scale = jnp.where(power == value - 3, 2.0 ** (value - 3), scale)
    spots = (4 * OWN, MODEL // 2)
    inside = lax.broadcasted_iota(jnp.int32, spots, 1) - HEAD * lax.broadcasted_iota(jnp.int32, spots, 0)
    spread = ((inside >= 0) & (inside < HEAD)).astype(BF16)
    scale = contract(scale.astype(BF16), spread, 0, 0)
    here = lax.broadcasted_iota(jnp.int32, scale.shape, 0) - 2 * c
    scale = [jnp.sum(jnp.where(here == r, scale, 0.0), axis=0, keepdims=True) for r in range(2)]
    for r in range(2):
        part = mraw[HEAD * r : HEAD * r + HEAD].astype(F32) * scale[r]
        wd[HEAD * r : HEAD * r + HEAD] = part.astype(BF16)
    pl.semaphore_wait(barrier, 2 * (LAYERS + BLOCKS) - 3)

    hid_local = pltpu.make_async_copy(cols(hid, zr), xbuf.at[0], hsem)
    hid_remote = push(cols(hid, zr), xbuf.at[0], sibsend.at[2], hsem, (z, c, 1))

    @pl.when((t == 1) & (zq == 1))
    def _():
        hid_local.start()

    @pl.when((t == 0) & (zq == 0))
    def _():
        hid_remote.start()

    for k in range(4):
        mine = (t == 1) & (zq == 1) & (zr == k)

        @pl.when(mine)
        def _():
            pltpu.make_async_copy(ld.at[k], graw.at[z], gsem.at[z]).start()

        @pl.when(jnp.logical_not(mine))
        def _():
            push(ld.at[k], graw.at[z], ldsend.at[k], gsem.at[z], (4 * t + k, c, 1)).start()

    @pl.when(t == 0)
    def _():
        distribute(z, c, y, zq, zr, push, arrived, sent, cols, wd, qk, wst, qst, wsrc, qsrc, wbuf, qbuf,
                   sibsem, zsend, zsem, psend, psem, rsend, wsem, qsem)

    @pl.when(t == 1)
    def _():
        @pl.when(z == 0)
        def _():
            for k in range(4):
                push(qk.at[k], qst.at[0], zsend.at[0, 4 + k], zsem.at[0, 0], (4 + k, c, 0)).start()
            for k in range(4):
                push(cols(wd, k), wst.at[0], zsend.at[1, 4 + k], zsem.at[1, 0], (4 + k, c, 0)).start()

        @pl.when(z > 0)
        def _():
            push(qk, qsrc, sibsend.at[0], sibsem.at[0], (z, c, 0)).start()
            push(wd, wsrc, sibsend.at[1], sibsem.at[1], (z, c, 0)).start()

        layers(z, c, zq, zr, push, arrived, sent, cols, hid_local, hid_remote, lens, out,
               xbuf, sbuf, nbuf, tbuf, wbuf, qbuf, graw, gbuf, cbuf, mbuf, allow, bits,
               gsem, csend, csem, ssend, ssem, tsend, tsem, nsend, nsem, osend, osem, wsem, qsem, nsem2)

        @pl.when(z == 0)
        def _():
            for k in range(4):
                sent(qk.at[k], zsend.at[0, 4 + k])
                sent(cols(wd, k), zsend.at[1, 4 + k])

        @pl.when(z > 0)
        def _():
            sent(qsrc, sibsend.at[0])
            sent(wsrc, sibsend.at[1])

    @pl.when((t == 0) & (zq == 0))
    def _():
        hid_remote.wait_send()

    for k in range(4):
        mine = (t == 1) & (zq == 1) & (zr == k)

        @pl.when(jnp.logical_not(mine))
        def _():
            sent(ld.at[k], ldsend.at[k])
            arrived(cols(out, k), osem.at[k])


def distribute(z, c, y, zq, zr, push, arrived, sent, cols, wd, qk, wst, qst, wsrc, qsrc, wbuf, qbuf,
               sibsem, zsend, zsem, psend, psem, rsend, wsem, qsem):
    x4 = c - y
    upper, lower = pl.ds(0, HEAD), pl.ds(HEAD, HEAD)

    def scatter(halves):
        for kind in range(2):
            for half in halves:
                if half:
                    arrived(wsrc if kind else qsrc, sibsem.at[kind])
                for k in range(4):
                    there = 4 * half + k
                    if kind == 0:
                        src = qsrc.at[k] if half else qk.at[k]
                        dst = qst.at[z]
                    else:
                        src = cols(wsrc if half else wd, k)
                        dst = wst.at[z]

                    @pl.when(z != there)
                    def _():
                        push(src, dst, zsend.at[kind, there], zsem.at[kind, z], (there, c, 0)).start()

                    @pl.when(z == there)
                    def _():
                        pltpu.make_async_copy(src, dst, zsem.at[kind, z]).start()

    def staged(kind, l, ref):
        @pl.when(z == l)
        def _():
            pltpu.make_async_copy(ref.at[l], ref.at[l], zsem.at[kind, l]).wait()

        @pl.when(z != l)
        def _():
            arrived(ref.at[l], zsem.at[kind, l])

    @pl.when(z == 0)
    def _():
        scatter((0,))

    def first_hop(l):
        staged(0, l, qst)
        for yy in range(4):
            push(qst.at[l], qbuf.at[l, y], rsend.at[l, 32 + yy], qsem.at[l], (z, x4 + yy, 1)).start()
        staged(1, l, wst)
        for d in range(1, 4):
            push(wst.at[l, upper], wbuf.at[l, c, upper], psend.at[l, 0, d], psem.at[l, 0, c // 4],
                 (z, lax.rem(c + 4 * d, BLOCKS), 0)).start()
            push(wst.at[l, lower], wbuf.at[l, c, lower], psend.at[l, 1, d], psem.at[l, 1, y],
                 (z, x4 + lax.rem(y + d, 4), 0)).start()

    def second_hop(l):
        for d in range(4):
            across = lax.rem(c + 4 * d, BLOCKS)
            along = x4 + lax.rem(y + d, 4)
            if d:
                arrived(wbuf.at[l, across, upper], psem.at[l, 0, across // 4])
                arrived(wbuf.at[l, along, lower], psem.at[l, 1, along - x4])
            for e in (2, 1, 3, 0):
                src = wbuf.at[l, across, upper] if d else wst.at[l, upper]
                push(src, wbuf.at[l, across, upper], rsend.at[l, 4 * d + e], wsem.at[l],
                     (z, x4 + lax.rem(y + e, 4), 1)).start()
                src = wbuf.at[l, along, lower] if d else wst.at[l, lower]
                push(src, wbuf.at[l, along, lower], rsend.at[l, 16 + 4 * d + e], wsem.at[l],
                     (z, lax.rem(c + 4 * e, BLOCKS), 1)).start()

    def step(l, carry):
        second_hop(l)

        @pl.when(l < LAYERS - 1)
        def _():
            first_hop(l + 1)

        return carry

    @pl.when(z > 0)
    def _():
        scatter((0, 1))

    first_hop(0)

    lax.fori_loop(0, LAYERS, step, 0)
    for there in range(LAYERS):

        @pl.when((z != there) & (z > 0) if there >= 4 else z != there)
        def _():
            sent(qst.at[z], zsend.at[0, there])
            sent(wst.at[z], zsend.at[1, there])

    def finish(l, carry):
        for e in range(4):
            sent(qst.at[l], rsend.at[l, 32 + e])
            for d in range(1, 4):
                if e < 2:
                    sent(wst.at[l, upper], psend.at[l, e, d])

        def one(e, inner):
            sent(wst.at[l, upper], rsend.at[l, e])
            return inner

        return lax.fori_loop(0, 32, one, carry)

    lax.fori_loop(0, LAYERS, finish, 0)


def layers(z, c, zq, zr, push, arrived, sent, cols, hid_local, hid_remote, lens, out,
           xbuf, sbuf, nbuf, tbuf, wbuf, qbuf, graw, gbuf, cbuf, mbuf, allow, bits,
           gsem, csend, csem, ssend, ssem, tsend, tsem, nsend, nsem, osend, osem, wsem, qsem, nsem2):
    e1 = lens[0, 0]
    e2 = e1 + lens[0, 1]
    e3 = e2 + lens[0, 2]

    def segment(p):
        return (p >= e1).astype(jnp.int32) + (p >= e2).astype(jnp.int32) + (p >= e3).astype(jnp.int32)

    first = c * ROWS
    seg_row = segment(first + lax.broadcasted_iota(jnp.int32, (ROWS, ROWS), 1))
    seg_col = segment(first + lax.broadcasted_iota(jnp.int32, (ROWS, ROWS), 0))
    later = lax.broadcasted_iota(jnp.int32, (ROWS, ROWS), 0) <= lax.broadcasted_iota(jnp.int32, (ROWS, ROWS), 1)
    small = first + lax.broadcasted_iota(jnp.int32, (8, ROWS), 1)
    seg_small = segment(small)
    seg_last = segment(jnp.full((8, ROWS), first + ROWS - 1, jnp.int32))
    before = jnp.where(c == 0, jnp.full((8, ROWS), -1, jnp.int32), segment(jnp.full((8, ROWS), first - 1, jnp.int32)))
    bits[0] = (seg_small == seg_last).astype(F32)
    bits[1] = (seg_small == before).astype(F32)
    bits[2] = (seg_last == before).astype(F32)
    lane8 = lax.broadcasted_iota(jnp.int32, (8, ROWS), 1)

    for l in range(LAYERS):
        mine = (zq == 1) & (z == l)

        @pl.when(mine)
        def _():
            pltpu.make_async_copy(graw.at[l], graw.at[l], gsem.at[l]).wait()

        @pl.when(jnp.logical_not(mine))
        def _():
            arrived(graw.at[l], gsem.at[l])

    g = graw[...].reshape(LAYERS * 8, ROWS)
    lane = lax.broadcasted_iota(jnp.int32, (LAYERS * 8, ROWS), 1)
    for s in (1, 2, 4, 8, 16, 32, 64):
        g = g + jnp.where(lane >= s, pltpu.roll(g, s, 1), 0.0)
    gbuf[...] = g.reshape(LAYERS, 8, ROWS)
    for l in range(LAYERS):
        kept = jnp.exp(jnp.broadcast_to(g[8 * l : 8 * l + 8, ROWS - 1 :], (8, ROWS))) * bits[2]
        cbuf[c, l] = jnp.where(lane8 < HEAD, kept, jnp.broadcast_to(kept[3:4], (8, ROWS)))

    def tell(there, carry):
        push(cbuf.at[c], cbuf.at[c], csend.at[there], csem.at[c], (z, there, 1)).start()
        return carry

    lax.fori_loop(c + 1, BLOCKS, tell, 0)
    allow[...] = jnp.where(later & (seg_row == seg_col), 0.0, -1e30)

    @pl.when(zq == 1)
    def _():
        hid_local.wait()

    @pl.when(zq == 0)
    def _():
        hid_remote.wait_recv()

    lane96 = lax.broadcasted_iota(jnp.int32, (HEAD, ROWS), 1)

    def emit(l):
        self_kept = (zq == 1) & (z == l)

        @pl.when(self_kept)
        def _():
            pltpu.make_async_copy(xbuf.at[l + 1], cols(out, zr), osem.at[zr]).start()

        @pl.when(jnp.logical_not(self_kept))
        def _():
            push(xbuf.at[l + 1], cols(out, zr), osend.at[l], osem.at[zr], (l, c, zq)).start()

    def emitted(l):
        self_kept = (zq == 1) & (z == l)

        @pl.when(self_kept)
        def _():
            pltpu.make_async_copy(xbuf.at[l + 1], cols(out, zr), osem.at[zr]).wait()

        @pl.when(jnp.logical_not(self_kept))
        def _():
            sent(xbuf.at[l + 1], osend.at[l])

    def gone(l):
        for slot in range(10):
            if slot in (4, 5, 8, 9):
                sent(nbuf.at[l, z], nsend.at[l, slot])
            else:
                sent(nbuf.at[l, z, pl.ds(0, ROWS // 2)], nsend.at[l, slot])

    def layer(l, carry):
        x = xbuf[l]
        xt = x.astype(F32).T
        own_squares = jnp.sum(xt * xt, axis=0, keepdims=True)
        sbuf[l, z] = own_squares
        for d in (4, 3, 5, 2, 6, 1, 7):
            push(sbuf.at[l, z], sbuf.at[l, z], ssend.at[l, d], ssem.at[l, z], (lax.rem(z + d, LAYERS), c, 1)).start()
        for h in range(OWN):
            row = jnp.broadcast_to(gbuf[l, h : h + 1], (ROWS, ROWS))
            mbuf[h] = jnp.exp(row - row.T + allow[...])

        @pl.when(l > 0)
        def _():
            gone(l - 1)

        arrived(qbuf.at[l], qsem.at[l])
        squares = own_squares
        for d in (1, 7, 2, 6, 3, 5, 4):
            there = lax.rem(z + d, LAYERS)
            arrived(sbuf.at[l, there], ssem.at[l, there])
            squares = squares + sbuf[l, there]
        xtb = (xt * lax.rsqrt(squares / MODEL + EPSILON)).astype(BF16)
        heads = [xtb[HEAD * h : HEAD * h + HEAD] for h in range(OWN)]
        raw = [contract(qbuf[l, h, HEAD:], heads[h], 1, 0) for h in range(OWN)]

        @pl.when(l > 0)
        def _():
            emit(l - 1)

        g = gbuf[l]
        key_scale = jnp.exp(jnp.broadcast_to(g[:, ROWS - 1 :], (8, ROWS)) - g) * bits[0]
        query_scale = jnp.exp(g) * bits[1]
        keys, values, keyed = [], [], []
        for h in range(OWN):
            k = jax.nn.silu(raw[h][:HEAD]).astype(BF16)
            keys.append(k)
            values.append(raw[h][HEAD:].astype(BF16))
            keyed.append((k.astype(F32) * key_scale[h : h + 1]).astype(BF16))
        for p in range(3):
            right = jnp.concatenate([keyed[p], keyed[3][32 * p : 32 * p + 32]], axis=0)
            both = contract(jnp.concatenate([values[p], values[3]], axis=0), right, 1, 1)
            tbuf[l, c, HEAD * p : HEAD * p + HEAD] = jnp.where(lane96 < HEAD, both[:HEAD], both[HEAD:]).astype(BF16)

        def states_out(there, carry):
            push(tbuf.at[l, c], tbuf.at[l, c], tsend.at[l, there], tsem.at[l, c], (z, there, 1)).start()
            return carry

        lax.fori_loop(c + 1, BLOCKS, states_out, 0)

        inner, queried = [], []
        for h in range(OWN):
            q = jax.nn.silu(contract(qbuf[l, h, :HEAD], heads[h], 1, 0)).astype(BF16)
            scores = contract(keys[h], q, 0, 0)
            weights = (scores * mbuf[h]).astype(BF16)
            inner.append(contract(values[h], weights, 1, 0))
            queried.append((q.astype(F32) * query_scale[h : h + 1]).astype(BF16))

        def fold(there, state):
            @pl.when(l == 0)
            def _():
                arrived(cbuf.at[there], csem.at[there])

            arrived(tbuf.at[l, there], tsem.at[l, there])
            return tuple(
                s * cbuf[there, l, p : p + 1] + tbuf[l, there, HEAD * p : HEAD * p + HEAD].astype(F32)
                for p, s in enumerate(state)
            )

        state = lax.fori_loop(0, c, fold, tuple(jnp.zeros((HEAD, ROWS), F32) for _ in range(3)))

        attended = list(inner)
        for p in range(3):
            left = jnp.concatenate([queried[p], jnp.zeros((32, ROWS), BF16)], axis=0)
            right = jnp.concatenate([jnp.zeros((HEAD, ROWS), BF16), queried[3][32 * p : 32 * p + 32]], axis=0)
            both = contract(state[p].astype(BF16), jnp.concatenate([left, right], axis=1), 1, 0)
            attended[p] = attended[p] + both[:, :ROWS]
            attended[3] = attended[3] + both[:, ROWS:]
        normed = [a * lax.rsqrt(jnp.mean(a * a, axis=0, keepdims=True) + EPSILON) for a in attended]
        nbuf[l, z] = jnp.concatenate(normed, axis=0).T.astype(BF16)
        def onward(source, rows, slot, d, sem=nsem):
            part = nbuf.at[l, source, rows]
            return push(part, part, nsend.at[l, slot], sem.at[l, source], (lax.rem(z + d, LAYERS), c, 1))

        every, early, late = pl.ds(0, ROWS), pl.ds(0, ROWS // 2), pl.ds(ROWS // 2, ROWS // 2)
        behind, ahead = lax.rem(z + 6, LAYERS), lax.rem(z + 2, LAYERS)
        onward(z, early, 0, 2).start()
        onward(z, late, 1, 6).start()
        onward(z, late, 2, 2, nsem2).start()
        onward(z, early, 3, 6, nsem2).start()
        onward(z, every, 4, 1).start()
        onward(z, every, 5, 7).start()

        def project(total, d):
            there = lax.rem(z + d, LAYERS)
            weight = wbuf[l, pl.ds(2 * there, 2)].reshape(WIDE, WIDE)
            return total + contract(nbuf[l, there], weight, 1, 0)

        def gathered(d):
            there = lax.rem(z + d, LAYERS)
            arrived(nbuf.at[l, there], nsem.at[l, there])

        for d in range(1, LAYERS):
            sent(sbuf.at[l, z], ssend.at[l, d])

        def states_sent(there, inner):
            sent(tbuf.at[l, c], tsend.at[l, there])
            return inner

        lax.fori_loop(c + 1, BLOCKS, states_sent, 0)
        arrived(wbuf.at[l], wsem.at[l])
        total = project(x.astype(F32), 0)
        for source, rows, slot, two in ((behind, early, 6, 2), (ahead, late, 7, 6)):
            arrived(nbuf.at[l, source, rows], nsem.at[l, source])
            onward(source, rows, slot, two).start()
        for source, rows, slot, one in ((behind, late, 8, 1), (ahead, early, 9, 7)):
            arrived(nbuf.at[l, source, rows], nsem2.at[l, source])
            onward(source, every, slot, one).start()
        for d in (1, 7, 2, 6, 3, 5, 4):
            if d not in (2, 6):
                gathered(d)
            total = project(total, d)

        xbuf[l + 1] = total.astype(BF16)
        return carry

    lax.fori_loop(0, LAYERS, layer, 0)
    emit(LAYERS - 1)

    gone(LAYERS - 1)

    def settle(l, carry):
        emitted(l)
        return carry

    lax.fori_loop(0, LAYERS, settle, 0)

    def told(there, carry):
        sent(cbuf.at[c], csend.at[there])
        return carry

    lax.fori_loop(c + 1, BLOCKS, told, 0)


def shards(hidden_in, qkv_weight, log_decay, lengths, out_mantissa, out_exponent):
    half = hidden_in.shape[2]
    dma = pltpu.SemaphoreType.DMA
    anywhere = pl.BlockSpec(memory_space=pl.ANY)
    outputs = pl.pallas_call(
        kernel,
        out_shape=jax.ShapeDtypeStruct((ROWS, half), BF16),
        in_specs=[anywhere] * 3 + [pl.BlockSpec(memory_space=pltpu.SMEM)] + [anywhere] * 2,
        out_specs=anywhere,
        scratch_shapes=[
            pltpu.VMEM((LAYERS + 1, ROWS, WIDE), BF16),
            pltpu.VMEM((LAYERS, LAYERS, 1, ROWS), F32),
            pltpu.VMEM((LAYERS, LAYERS, ROWS, WIDE), BF16),
            pltpu.VMEM((LAYERS, BLOCKS, 3 * HEAD, ROWS), BF16),
            pltpu.VMEM((LAYERS, BLOCKS, 2 * HEAD, WIDE), BF16),
            pltpu.VMEM((LAYERS, OWN, 3 * HEAD, HEAD), BF16),
            pltpu.VMEM((LAYERS, 8, ROWS), F32),
            pltpu.VMEM((LAYERS, 8, ROWS), F32),
            pltpu.VMEM((BLOCKS, LAYERS, 8, ROWS), F32),
            pltpu.VMEM((OWN, ROWS, ROWS), F32),
            pltpu.VMEM((ROWS, ROWS), F32),
            pltpu.VMEM((LAYERS, 2 * HEAD, WIDE), BF16),
            pltpu.VMEM((LAYERS, 3 * HEAD, HEAD), BF16),
            pltpu.VMEM((2 * HEAD, half), BF16),
            pltpu.VMEM((4, 3 * HEAD, HEAD), BF16),
            pltpu.VMEM((3, 8, ROWS), F32),
            dma((4,)),
            dma,
            dma((3,)),
            dma((2,)),
            dma((LAYERS,)),
            dma((BLOCKS,)),
            dma((BLOCKS,)),
            dma((LAYERS, LAYERS)),
            dma((LAYERS, LAYERS)),
            dma((LAYERS, BLOCKS)),
            dma((LAYERS, BLOCKS)),
            dma((LAYERS, 10)),
            dma((LAYERS, LAYERS)),
            dma((LAYERS,)),
            dma((4,)),
            dma((2, LAYERS)),
            dma((2, LAYERS)),
            dma((LAYERS, 2, 4)),
            dma((LAYERS, 2, 4)),
            dma((LAYERS, 36)),
            dma((LAYERS,)),
            dma((LAYERS,)),
            dma((LAYERS, LAYERS)),
            pltpu.VMEM((2 * HEAD, half), BF16),
            pltpu.VMEM((4, 3 * HEAD, HEAD), BF16),
            pltpu.VMEM((4, 8, ROWS), F32),
            pltpu.VMEM((2 * HEAD, half), BF16),
            pltpu.VMEM((4, HEAD, 3 * HEAD), BF16),
            pltpu.VMEM((4 * OWN, ROWS), F32),
            pltpu.VMEM((4 * OWN, 2 * OWN * 4), jnp.int32),
            dma((7,)),
        ],
        compiler_params=pltpu.CompilerParams(collective_id=0, has_side_effects=True, vmem_limit_bytes=58 << 20),
    )(hidden_in[0], qkv_weight[0], log_decay[0, 0].T, lengths, out_mantissa[0], out_exponent[0].T)
    return outputs[None, None]


def solution(mesh):
    in_specs = (
        P(None, "ctx", "tp"),
        P("phase", "tp", None, None),
        P("phase", None, "ctx", "tp"),
        P(),
        P("phase", "ctx", "tp"),
        P("phase", None, "tp"),
    )
    out_specs = P("phase", None, "ctx", "tp")
    return jax.shard_map(shards, mesh=mesh, in_specs=in_specs, out_specs=out_specs, check_vma=False)
```
